256 devices in a mesh: head: 8 (over x_lo, y), blk: 32 (over z, x_hi, core).
Axes of the slice: x: 4 (x_hi: 2, x_lo: 2; x = x_hi * 2 + x_lo), y: 4, z: 8, core: 2. Of those that a mesh axis runs over, the one named last changes fastest.
Arguments:
- queries: bfloat16 [8192, 4096], P(('head', 'blk')), may hold values from -6 to 6
- key_heads: bfloat16 [8192, 512], P(('head', 'blk')), may hold values from -6 to 6
- value_heads: bfloat16 [8192, 512], P(('head', 'blk')), may hold values from -6 to 6
- outputs: bfloat16 [8192, 4096], P(('head', 'blk')), may hold values from -6 to 6
- out_grad: bfloat16 [8192, 4096], P(('head', 'blk')), may hold values from -6 to 6
- log_total: bfloat16 [8192, 32], P(('head', 'blk')), may hold values from 0 to 20
- positions: int32 [32, 256], replicated, may hold values from 0 to 8191, as said below
Outputs:
- query_grad: bfloat16 [8192, 4096], P(('head', 'blk'))
- key_grad: bfloat16 [8192, 512], P(('head', 'blk'))
- value_grad: bfloat16 [8192, 512], P(('head', 'blk'))
The draws below stay inside these ranges and needn't reach their ends.
Inputs may be any that keep to these rules, and one draw needn't show every extreme that they name: Every position 0 to 8191 appears once. Each row of positions is two runs of 128 consecutive rising positions, each run starting at a multiple of its length.
All inputs are finite; a program needn't handle non-finite values.
Results may differ from the reference program's by a relative error of at most 0.012.
Values may be sent and summed in bfloat16 or wider, within the bound.
A program may use at most 64 MiB of HBM per device.

```python
import math
import jax
import jax.numpy as jnp
from jax import lax

D = 128
GROUP = 8
HQ = 32
TOK_DEV = 32
KVH = 4
TOKENS = 8192
N_HEAD = 8
N_BLK = 32


def position_table(key):
    key = jax.random.fold_in(key, 11)
    runs = jax.random.permutation(key, 2 * N_BLK).astype(jnp.int32)
    width = TOK_DEV * N_HEAD
    run_len = width // 2
    columns = jnp.arange(width, dtype=jnp.int32)
    starts = runs.reshape(N_BLK, 2)[:, columns // run_len]
    return (starts * run_len + columns % run_len).astype(jnp.int32)


def draw_positions(key, part):
    return position_table(key)


def draw_log_total(key, part):
    table = position_table(key)
    key = jax.random.fold_in(key, 13)
    seq_pos = table.reshape(N_BLK, N_HEAD, TOK_DEV).transpose(1, 0, 2).reshape(TOKENS)
    base = jnp.log(seq_pos.astype(jnp.float32) + 1.0) + 0.5
    offset = jax.random.uniform(key, (TOKENS, HQ), jnp.float32, -0.5, 0.5)
    return (base[:, None] + offset).astype(jnp.bfloat16)


def shard_levels(own_key, extent, split, least, high):
    level = 1.0
    for dim, parts in split:
        heights = jax.random.uniform(jax.random.fold_in(jax.random.fold_in(own_key, 6), dim), (parts,), jnp.float32, least / len(split), high / len(split))
        level = level * jnp.repeat(jnp.exp(heights), extent[dim] // parts).reshape((-1,) + (1,) * (len(extent) - 1 - dim))
    return level


def noise(stream_key, shape, spread, bound, shards=(), kind=jnp.bfloat16):
    entries = jax.random.normal(stream_key, shape, jnp.float32) * spread
    if len(shards) > 0:
        entries = shard_levels(stream_key, shape, shards, -0.22, 0.18) * entries
    return jnp.clip(entries, min=-bound, max=bound).astype(kind)


def setup_inputs(seed: int = 0) -> dict:
    splits = jax.random.split(jax.random.key(seed), 8)
    return {
        "queries": noise(splits[0], (TOKENS, HQ * D), 1.0, 6.0, ((0, 256),)),
        "key_heads": noise(splits[1], (TOKENS, KVH * D), 1.0, 6.0, ((0, 256),)),
        "value_heads": noise(splits[2], (TOKENS, KVH * D), 1.0, 6.0, ((0, 256),)),
        "outputs": noise(splits[3], (TOKENS, HQ * D), 1.0, 6.0, ((0, 256),)),
        "out_grad": noise(splits[4], (TOKENS, HQ * D), 1.0, 6.0, ((0, 256),)),
        "log_total": draw_log_total(jax.random.fold_in(splits[7], 71), 0),
        "positions": draw_positions(jax.random.fold_in(splits[7], 71), 0),
    }


def reference(queries, key_heads, value_heads, outputs, out_grad, log_total, positions):
    flat_pos = positions.reshape(N_BLK, N_HEAD, TOK_DEV).transpose(1, 0, 2).reshape(TOKENS)
    order = jnp.argsort(flat_pos).astype(jnp.int32)
    inverse = jnp.argsort(order).astype(jnp.int32)
    block = min(512, TOKENS)
    blocks = TOKENS // block
    scale = 1.0 / math.sqrt(D)
    kv_count = HQ // GROUP
    query_all = queries[order].reshape(TOKENS, HQ, D).transpose(1, 0, 2)
    grad_all = out_grad[order].reshape(TOKENS, HQ, D).transpose(1, 0, 2)
    key_all = key_heads[order].reshape(TOKENS, kv_count, D).transpose(1, 0, 2)
    value_all = value_heads[order].reshape(TOKENS, kv_count, D).transpose(1, 0, 2)
    log_all = log_total[order].astype(jnp.float32).T
    delta_all = lax.optimization_barrier(jnp.sum(outputs[order].astype(jnp.float32).reshape(TOKENS, HQ, D) * out_grad[order].astype(jnp.float32).reshape(TOKENS, HQ, D), axis=2)).T
    lower = jnp.arange(block)[:, None] >= jnp.arange(block)[None, :]
    indices = jnp.arange(blocks, dtype=jnp.int32)

    def piece(array, index):
        return lax.dynamic_slice_in_dim(array, (index * block).astype(jnp.int32), block, 0)

    def head_terms(head):
        group = head // GROUP
        query_h = query_all[head]
        grad_h = grad_all[head]
        delta_h = delta_all[head]
        log_h = log_all[head]
        key_g = key_all[group]
        value_g = value_all[group]

        def visible(row_index, col_index):
            return jnp.logical_or(row_index > col_index, lower)

        def scores_of(row_index, col_index):
            return jnp.dot(piece(query_h, row_index), piece(key_g, col_index).T, preferred_element_type=jnp.float32) * scale

        def key_column(query_acc, col_index):

            def step(row_index, carry):
                key_acc, value_acc, query_inner = carry
                scores = scores_of(row_index, col_index)
                mask = visible(row_index, col_index)
                probs = jnp.where(mask, jnp.exp(scores - piece(log_h, row_index)[:, None]), 0.0)
                grad_block = piece(grad_h, row_index)
                value_acc = value_acc + jnp.dot(probs.astype(jnp.bfloat16).T, grad_block, preferred_element_type=jnp.float32)
                prob_grad = jnp.dot(grad_block, piece(value_g, col_index).T, preferred_element_type=jnp.float32)
                score_grad = (probs * (prob_grad - piece(delta_h, row_index)[:, None])).astype(jnp.bfloat16)
                key_acc = key_acc + jnp.dot(score_grad.T, piece(query_h, row_index), preferred_element_type=jnp.float32) * scale
                query_term = jnp.dot(score_grad, piece(key_g, col_index), preferred_element_type=jnp.float32) * scale
                query_inner = lax.dynamic_update_slice_in_dim(query_inner, piece(query_inner, row_index) + query_term, (row_index * block).astype(jnp.int32), 0)
                return (key_acc, value_acc, query_inner)
            empty = jnp.zeros((block, D), jnp.float32)
            key_acc, value_acc, query_acc = lax.fori_loop(col_index, jnp.int32(blocks), step, (empty, empty, query_acc))
            return (query_acc, (key_acc, value_acc))
        query_grad, kv_terms = lax.scan(key_column, jnp.zeros((TOKENS, D), jnp.float32), indices)
        return (query_grad, kv_terms[0].reshape(TOKENS, D), kv_terms[1].reshape(TOKENS, D))
    query_grad, key_grad, value_grad = lax.map(head_terms, jnp.arange(HQ, dtype=jnp.int32))
    key_grad = key_grad.reshape(kv_count, GROUP, TOKENS, D).sum(axis=1)
    value_grad = value_grad.reshape(kv_count, GROUP, TOKENS, D).sum(axis=1)
    query_out = query_grad.transpose(1, 0, 2).reshape(TOKENS, HQ * D)[inverse].astype(jnp.bfloat16)
    key_out = key_grad.transpose(1, 0, 2).reshape(TOKENS, kv_count * D)[inverse].astype(jnp.bfloat16)
    value_out = value_grad.transpose(1, 0, 2).reshape(TOKENS, kv_count * D)[inverse].astype(jnp.bfloat16)
    return (query_out, key_out, value_out)
```

```python
import math

import jax
import jax.numpy as jnp
from jax import lax
from jax.experimental import pallas as pl
from jax.experimental.pallas import tpu as pltpu
from jax.sharding import PartitionSpec as P

D = 128
GROUP = 8
HQ = 32
KVH = 4
TOK = 32
PLANE = 32
Q_ROWS = PLANE * TOK
PART = 256
RUN = 128
Z = 8
LOCAL = 4
QT = 256
SCALE = 1.0 / math.sqrt(D)
EXP2_SCALE = SCALE * math.log2(math.e)
BF = jnp.bfloat16
F32 = jnp.float32
MESH = pl.DeviceIdType.MESH


def pieces_of(value):
    high = value.astype(BF)
    rest = value - high.astype(F32)
    mid = rest.astype(BF)
    low = (rest - mid.astype(F32)).astype(BF)
    return high, mid, low


def kernel(
    q_ref,
    k_ref,
    v_ref,
    o_ref,
    g_ref,
    lse_ref,
    pos_ref,
    dq_out,
    dk_out,
    dv_out,
    pack0,
    pack1,
    qd,
    qt,
    gt,
    auxt,
    qpos,
    kv,
    acc,
    dqt,
    dqs,
    rs_send,
    rs,
    dq_recv,
    kv_recv,
    q_send_sem,
    q_recv_sem,
    fwd_send_sem,
    fwd_recv_sem,
    kv_send_sem,
    kv_recv_sem,
    ring_send_sem,
    ring_recv_sem,
    rs_send_sem,
    rs_recv_sem,
    dq_send_sem,
    dq_recv_sem,
    out_send_sem,
    out_recv_sem,
):
    h = lax.axis_index("head")
    b = lax.axis_index("blk")
    z = b // 4
    x_hi = (b // 2) % 2
    core = b % 2
    x_lo = h // 4
    y = h % 4
    me = (b % 4) * 8 + h
    right = (h, (b + 4) % 32)
    left = (h, (b + 28) % 32)
    sibling = (h, z * 4 + x_hi * 2 + (1 - core))

    def plane_device(p):
        return (p % 8, z * 4 + p // 8)

    barrier = pltpu.get_barrier_semaphore()

    def greet(i, carry):
        pl.semaphore_signal(
            barrier, inc=1, device_id=plane_device((me + i) % PLANE), device_id_type=MESH
        )
        return carry

    lax.fori_loop(1, PLANE, greet, 0)
    pl.semaphore_signal(barrier, inc=1, device_id=right, device_id_type=MESH)
    pl.semaphore_signal(barrier, inc=1, device_id=left, device_id_type=MESH)

    lane32 = lax.broadcasted_iota(jnp.int32, (TOK, HQ), 1)
    delta = jnp.zeros((TOK, HQ), F32)
    for head in range(HQ):
        cols = slice(head * D, (head + 1) * D)
        term = jnp.sum(
            g_ref[:, cols].astype(F32) * o_ref[:, cols].astype(F32), axis=1, keepdims=True
        )
        delta = jnp.where(lane32 == head, term, delta)
    aux_all = jnp.zeros((TOK, HQ // LOCAL * D), F32)
    sel_row = lax.broadcasted_iota(jnp.int32, (HQ, HQ // LOCAL * D), 0)
    sel_col = lax.broadcasted_iota(jnp.int32, (HQ, HQ // LOCAL * D), 1)
    sel_base = (sel_row // LOCAL) * D + 6 * (sel_row % LOCAL)
    parts = pieces_of(lse_ref[...].astype(F32) * (-math.sqrt(D))) + pieces_of(-delta)
    for index, part in enumerate(parts):
        place = jnp.where(sel_col == sel_base + index, 1.0, 0.0).astype(BF)
        aux_all = aux_all + jnp.dot(part, place, preferred_element_type=F32)
    aux_low = aux_all.astype(BF)
    for hh in range(2):
        for c in range(2):
            for g in range(4):
                slot = (hh * 2 + c) * 4 + g
                head = g * 8 + hh * 4 + 2 * c
                pack0[slot, :, 0:D] = q_ref[:, head * D : (head + 1) * D]
                pack0[slot, :, D : 2 * D] = g_ref[:, head * D : (head + 1) * D]
                pack0[slot, :, 2 * D : 3 * D] = aux_low[:, (g * 2 + hh) * D : (g * 2 + hh + 1) * D]
                pack1[slot, :, 0:D] = q_ref[:, (head + 1) * D : (head + 2) * D]
                pack1[slot, :, D : 2 * D] = g_ref[:, (head + 1) * D : (head + 2) * D]

    pl.semaphore_wait(barrier, PLANE + 1)

    key_rows = pl.ds(pl.multiple_of(x_hi * RUN + y * TOK, TOK), TOK)
    my_j = x_hi * 4 + y

    def part_device(j):
        return (x_lo * 4 + j % 4, z * 4 + (j // 4) * 2 + core)

    def kv_copy(i, which):
        j = (my_j + i) % 8
        src = (k_ref, v_ref)[which]
        cols = pl.ds(pl.multiple_of((j % 4) * D, D), D)
        return pltpu.make_async_remote_copy(
            src_ref=src.at[:, cols],
            dst_ref=kv.at[0, which, key_rows, :],
            send_sem=kv_send_sem.at[which, i],
            recv_sem=kv_recv_sem,
            device_id=part_device(j),
            device_id_type=MESH,
        )

    def kv_local(which):
        src = (k_ref, v_ref)[which]
        cols = pl.ds(pl.multiple_of(y * D, D), D)
        return pltpu.make_async_copy(src.at[:, cols], kv.at[0, which, key_rows, :], kv_recv_sem)

    def kv_start(i, carry):
        kv_copy(i, 0).start()
        kv_copy(i, 1).start()
        return carry

    lax.fori_loop(1, 8, kv_start, 0)
    kv_local(0).start()
    kv_local(1).start()

    q_rows = pl.ds(pl.multiple_of(me * TOK, TOK), TOK)

    def q_copy(stage, i):
        p = (me + i) % PLANE
        slot = (p // 8) * 4 + p % 4
        if stage == 0:
            src, dst = pack0.at[slot], qd.at[0, q_rows, :]
        else:
            src, dst = pack1.at[slot], qd.at[2, q_rows, 0 : 2 * D]
        return pltpu.make_async_remote_copy(
            src_ref=src,
            dst_ref=dst,
            send_sem=q_send_sem.at[stage, i],
            recv_sem=q_recv_sem.at[stage],
            device_id=plane_device(p),
            device_id_type=MESH,
        )

    own_slot = (me // 8) * 4 + me % 4

    def q_start(stage):
        def body(i, carry):
            q_copy(stage, i).start()
            return carry

        lax.fori_loop(1, PLANE, body, 0)

    q_start(0)
    pltpu.make_async_copy(pack0.at[own_slot], qd.at[0, q_rows, :], q_recv_sem.at[0]).start()
    q_start(1)
    pltpu.make_async_copy(
        pack1.at[own_slot], qd.at[2, q_rows, 0 : 2 * D], q_recv_sem.at[1]
    ).start()

    run_iota = lax.broadcasted_iota(jnp.int32, (1, RUN), 1)
    for r in range(8):
        qpos[0:1, r * RUN : (r + 1) * RUN] = run_iota + pos_ref[z * 4 + r // 2, (r % 2) * RUN]

    def ring_copy(src, dst, device):
        return pltpu.make_async_remote_copy(
            src_ref=kv.at[src],
            dst_ref=kv.at[dst],
            send_sem=ring_send_sem.at[dst],
            recv_sem=ring_recv_sem.at[dst],
            device_id=device,
            device_id_type=MESH,
        )

    def ring_step(i):
        @pl.when(i < 3)
        def _():
            ring_copy(i, i + 1, left).wait_recv()

            @pl.when(i < 2)
            def _():
                ring_copy(i + 1, i + 2, left).start()

        ring_copy((8 - i) % 8, 7 - i, right).wait_recv()

        @pl.when(i < 3)
        def _():
            ring_copy(7 - i, 6 - i, right).start()

    pltpu.make_async_copy(kv.at[0], kv.at[0], kv_recv_sem).wait()
    ring_copy(0, 7, right).start()
    ring_copy(0, 1, left).start()

    aux_row = lax.broadcasted_iota(jnp.int32, (D, QT), 0)
    ones = jnp.ones((2 * PART, D), BF)

    def local_head(n):
        own = core if n % 2 == 0 else 1 - core
        return 2 * own + n // 2

    def prepare(n):
        buf = n % 2
        first = 6 * local_head(n)
        for r in range(0, Q_ROWS, QT):
            cols = slice(r, r + QT)
            qt[buf, 0:D, cols] = qd[n, cols, 0:D].T
            gt[buf, 0:D, cols] = qd[n, cols, D : 2 * D].T
            if n == 0:
                auxt[:, cols] = qd[0, cols, 2 * D : 3 * D].T
            aux = auxt[:, cols]
            empty = jnp.zeros_like(aux)
            qt[buf, D : 2 * D, cols] = jnp.where(
                (aux_row >= first) & (aux_row < first + 3), aux, empty
            )
            gt[buf, D : 2 * D, cols] = jnp.where(
                (aux_row >= first + 3) & (aux_row < first + 6), aux, empty
            )
        dqt[buf] = jnp.zeros((D, Q_ROWS), F32)

    key_iota = lax.broadcasted_iota(jnp.int32, (RUN, QT), 0)

    def attend(heads, a, c):
        keys = jnp.concatenate([kv[a, 0], kv[c, 0]], axis=0)
        values = jnp.concatenate([kv[a, 1], kv[c, 1]], axis=0)
        keys_wide = jnp.concatenate([keys, ones], axis=1)
        values_wide = jnp.concatenate([values, ones], axis=1)
        keys_t = keys.T
        starts = []
        for j in range(4):
            slot = a if j < 2 else c
            row = ((z + slot) % Z) * 4 + (j % 2) * 2 + core
            starts.append(pos_ref[row, x_lo * RUN])
        dk = jnp.zeros((2 * PART, D), F32)
        dv = jnp.zeros((2 * PART, D), F32)
        for n in heads:
            buf = n % 2
            for r in range(0, Q_ROWS, QT):
                cols = slice(r, r + QT)
                scores = jnp.dot(keys_wide, qt[buf, :, cols], preferred_element_type=F32)
                shifted = jnp.dot(values_wide, gt[buf, :, cols], preferred_element_type=F32)
                raw = jnp.exp2(scores * EXP2_SCALE)
                where = qpos[0:1, cols]
                probs = jnp.concatenate(
                    [
                        jnp.where(
                            where - starts[j] >= key_iota, raw[j * RUN : (j + 1) * RUN], 0.0
                        )
                        for j in range(4)
                    ],
                    axis=0,
                )
                score_grad = (probs * shifted).astype(BF)
                dv = dv + jnp.dot(
                    probs.astype(BF), qd[n, cols, D : 2 * D], preferred_element_type=F32
                )
                dk = dk + jnp.dot(score_grad, qd[n, cols, 0:D], preferred_element_type=F32)
                dqt[buf, :, cols] += jnp.dot(keys_t, score_grad, preferred_element_type=F32)
        return dk, dv

    def slots_of(i):
        return (8 - i) % 8, i + 1

    quarter = x_lo * 2 + core

    def dq_columns(n):
        head = y * 8 + x_hi * 4 + local_head(n)
        return pl.ds(pl.multiple_of(head * D, D), D)

    def dq_copy(n, i):
        p = (me + i) % PLANE
        return pltpu.make_async_remote_copy(
            src_ref=dqs.at[n, pl.ds(pl.multiple_of(p * TOK, TOK), TOK), :],
            dst_ref=dq_recv.at[quarter, :, dq_columns(n)],
            send_sem=dq_send_sem.at[n, i],
            recv_sem=dq_recv_sem,
            device_id=plane_device(p),
            device_id_type=MESH,
        )

    def send_dq(n):
        for r in range(0, Q_ROWS, QT):
            dqs[n, r : r + QT, :] = (dqt[n % 2, :, r : r + QT] * SCALE).T.astype(BF)

        def body(i, carry):
            dq_copy(n, i).start()
            return carry

        lax.fori_loop(1, PLANE, body, 0)
        pltpu.make_async_copy(
            dqs.at[n, q_rows, :], dq_recv.at[quarter, :, dq_columns(n)], dq_recv_sem
        ).start()

    def forward(stage):
        return pltpu.make_async_remote_copy(
            src_ref=qd.at[2 * stage, :, 0 : 2 * D],
            dst_ref=qd.at[2 * stage + 1, :, 0 : 2 * D],
            send_sem=fwd_send_sem.at[stage],
            recv_sem=fwd_recv_sem.at[stage],
            device_id=sibling,
            device_id_type=MESH,
        )

    ring_step(0)
    pltpu.make_async_copy(qd.at[0], qd.at[0], q_recv_sem.at[0]).wait()
    forward(0).start()
    prepare(0)

    def first_head(i, carry):
        @pl.when(i < 3)
        def _():
            ring_step(i + 1)

        a, c = slots_of(i)
        dk, dv = attend((0,), a, c)
        acc[a, 0] = dk[:PART]
        acc[c, 0] = dk[PART:]
        acc[a, 1] = dv[:PART]
        acc[c, 1] = dv[PART:]
        return carry

    lax.fori_loop(0, 4, first_head, 0)
    send_dq(0)

    forward(0).wait_recv()
    prepare(1)

    def second_head(i, carry):
        a, c = slots_of(i)
        dk, dv = attend((1,), a, c)
        acc[a, 0] += dk[:PART]
        acc[c, 0] += dk[PART:]
        acc[a, 1] += dv[:PART]
        acc[c, 1] += dv[PART:]
        return carry

    lax.fori_loop(0, 4, second_head, 0)
    send_dq(1)

    pltpu.make_async_copy(
        qd.at[2, :, 0 : 2 * D], qd.at[2, :, 0 : 2 * D], q_recv_sem.at[1]
    ).wait()
    forward(1).start()
    prepare(2)
    forward(1).wait_recv()
    prepare(3)

    def rs_copy(src, dst, device):
        return pltpu.make_async_remote_copy(
            src_ref=rs_send.at[src],
            dst_ref=rs.at[dst],
            send_sem=rs_send_sem.at[dst],
            recv_sem=rs_recv_sem.at[dst],
            device_id=device,
            device_id_type=MESH,
        )

    def last_heads(step, carry):
        i = 3 - step
        a, c = slots_of(i)
        dk, dv = attend((2, 3), a, c)
        acc[a, 0] += dk[:PART]
        acc[c, 0] += dk[PART:]
        acc[a, 1] += dv[:PART]
        acc[c, 1] += dv[PART:]

        @pl.when(step > 0)
        def _():
            rs_copy(c + 1, c, right).wait_recv()
            acc[c] += rs[c].astype(F32)

        rs_send[c] = acc[c].astype(BF)
        rs_copy(c, c - 1, right).start()

        @pl.when((step > 0) & (step < 3))
        def _():
            rs_copy(a - 1, a, left).wait_recv()
            acc[a] += rs[a].astype(F32)

        @pl.when(step < 2)
        def _():
            rs_send[a] = acc[a].astype(BF)
            rs_copy(a, a + 1, left).start()

        @pl.when(step == 2)
        def _():
            rs_send[7] = acc[7].astype(BF)
            rs_copy(7, 4, left).start()

        return carry

    lax.fori_loop(0, 4, last_heads, 0)
    send_dq(2)
    send_dq(3)

    rs_copy(7, 4, left).wait_recv()
    rs_copy(1, 0, right).wait_recv()
    rs_send[0] = (acc[0] + rs[4].astype(F32) + rs[0].astype(F32)).astype(BF)

    out_cols = pl.ds(pl.multiple_of(y * D, D), D)

    def out_copy(i, which):
        j = (my_j + i) % 8
        rows = pl.ds(pl.multiple_of((j // 4) * RUN + (j % 4) * TOK, TOK), TOK)
        return pltpu.make_async_remote_copy(
            src_ref=rs_send.at[0, which, rows, :],
            dst_ref=kv_recv.at[x_hi, which, :, out_cols],
            send_sem=out_send_sem.at[which, i],
            recv_sem=out_recv_sem,
            device_id=part_device(j),
            device_id_type=MESH,
        )

    def out_start(i, carry):
        out_copy(i, 0).start()
        out_copy(i, 1).start()
        return carry

    lax.fori_loop(1, 8, out_start, 0)
    for which in range(2):
        pltpu.make_async_copy(
            rs_send.at[0, which, key_rows, :], kv_recv.at[x_hi, which, :, out_cols], out_recv_sem
        ).start()

    pltpu.make_async_copy(dq_recv, dq_recv, dq_recv_sem).wait()
    for r in range(0, HQ * D, 512):
        cols = slice(r, r + 512)
        total = dq_recv[0, :, cols].astype(F32) + dq_recv[1, :, cols].astype(F32)
        total = total + dq_recv[2, :, cols].astype(F32) + dq_recv[3, :, cols].astype(F32)
        dq_out[:, cols] = total.astype(BF)
    pltpu.make_async_copy(kv_recv, kv_recv, out_recv_sem).wait()
    dk_out[...] = ((kv_recv[0, 0].astype(F32) + kv_recv[1, 0].astype(F32)) * SCALE).astype(BF)
    dv_out[...] = (kv_recv[0, 1].astype(F32) + kv_recv[1, 1].astype(F32)).astype(BF)

    def finish_plane(i, carry):
        q_copy(0, i).wait_send()
        q_copy(1, i).wait_send()
        for n in range(LOCAL):
            dq_copy(n, i).wait_send()
        return carry

    lax.fori_loop(1, PLANE, finish_plane, 0)

    def finish_part(i, carry):
        for which in range(2):
            kv_copy(i, which).wait_send()
            out_copy(i, which).wait_send()
        return carry

    lax.fori_loop(1, 8, finish_part, 0)
    forward(0).wait_send()
    forward(1).wait_send()
    for dst in range(1, 8):
        ring_copy(0, dst, right).wait_send()
    for dst in (0, 1, 2, 3, 4, 6, 7):
        rs_copy(0, dst, right).wait_send()


def shards(queries, key_heads, value_heads, outputs, out_grad, log_total, positions):
    vmem = pl.BlockSpec(memory_space=pltpu.VMEM)
    smem = pl.BlockSpec(memory_space=pltpu.SMEM)
    dma = pltpu.SemaphoreType.DMA
    return pl.pallas_call(
        kernel,
        out_shape=(
            jax.ShapeDtypeStruct((TOK, HQ * D), BF),
            jax.ShapeDtypeStruct((TOK, KVH * D), BF),
            jax.ShapeDtypeStruct((TOK, KVH * D), BF),
        ),
        in_specs=[vmem] * 6 + [smem],
        out_specs=(vmem, vmem, vmem),
        scratch_shapes=[
            pltpu.VMEM((16, TOK, 3 * D), BF),
            pltpu.VMEM((16, TOK, 2 * D), BF),
            pltpu.VMEM((LOCAL, Q_ROWS, 3 * D), BF),
            pltpu.VMEM((2, 2 * D, Q_ROWS), BF),
            pltpu.VMEM((2, 2 * D, Q_ROWS), BF),
            pltpu.VMEM((D, Q_ROWS), BF),
            pltpu.VMEM((8, Q_ROWS), jnp.int32),
            pltpu.VMEM((Z, 2, PART, D), BF),
            pltpu.VMEM((Z, 2, PART, D), F32),
            pltpu.VMEM((2, D, Q_ROWS), F32),
            pltpu.VMEM((LOCAL, Q_ROWS, D), BF),
            pltpu.VMEM((Z, 2, PART, D), BF),
            pltpu.VMEM((Z, 2, PART, D), BF),
            pltpu.VMEM((4, TOK, HQ * D), BF),
            pltpu.VMEM((2, 2, TOK, KVH * D), BF),
            dma((2, PLANE)),
            dma((2,)),
            dma((2,)),
            dma((2,)),
            dma((2, 8)),
            dma,
            dma((Z,)),
            dma((Z,)),
            dma((Z,)),
            dma((Z,)),
            dma((LOCAL, PLANE)),
            dma,
            dma((2, 8)),
            dma,
        ],
        compiler_params=pltpu.CompilerParams(
            collective_id=0, has_side_effects=True, vmem_limit_bytes=50 << 20
        ),
    )(queries, key_heads, value_heads, outputs, out_grad, log_total, positions)


def solution(mesh):
    spec = P(("head", "blk"), None)
    return jax.shard_map(
        shards,
        mesh=mesh,
        in_specs=(spec,) * 6 + (P(),),
        out_specs=(spec,) * 3,
        check_vma=False,
    )
```

```python
import math

import jax
import jax.numpy as jnp
from jax import lax
from jax.experimental import pallas as pl
from jax.experimental.pallas import tpu as pltpu
from jax.sharding import PartitionSpec as P

D = 128
HQ = 32
KVH = 4
TOK = 32
SUB = TOK // 2
PLANE = 32
HALF = PLANE * SUB
Q_ROWS = 2 * HALF
PART = 256
RUN = 128
Z = 8
LOCAL = 4
QT = 256
SCALE = 1.0 / math.sqrt(D)
EXP2_SCALE = SCALE * math.log2(math.e)
BF = jnp.bfloat16
F32 = jnp.float32
MESH = pl.DeviceIdType.MESH


def pieces_of(value):
    high = value.astype(BF)
    rest = value - high.astype(F32)
    mid = rest.astype(BF)
    low = (rest - mid.astype(F32)).astype(BF)
    return high, mid, low


def kernel(
    q_hbm,
    k_hbm,
    v_hbm,
    o_hbm,
    g_hbm,
    lse_hbm,
    pos_hbm,
    dq_out,
    dk_out,
    dv_out,
    q_ref,
    k_ref,
    v_ref,
    o_ref,
    g_ref,
    lse_ref,
    pos_ref,
    pack,
    pack_aux,
    qd,
    aux,
    auxt,
    qt,
    gt,
    qpos,
    kv,
    acc,
    dqt,
    dqs,
    dqx_send,
    dqx,
    rs_send,
    rs,
    dq_recv,
    kv_recv,
    in_sem,
    q_send_sem,
    q_recv_sem,
    fwd_send_sem,
    fwd_recv_sem,
    kv_send_sem,
    kv_recv_sem,
    ring_send_sem,
    ring_recv_sem,
    rs_send_sem,
    rs_recv_sem,
    dqx_send_sem,
    dqx_recv_sem,
    dq_send_sem,
    dq_recv_sem,
    out_send_sem,
    out_recv_sem,
):
    loads = [
        pltpu.make_async_copy(src, dst, in_sem.at[index])
        for index, (src, dst) in enumerate(
            [
                (g_hbm, g_ref),
                (o_hbm, o_ref),
                (lse_hbm, lse_ref),
                (q_hbm, q_ref),
                (k_hbm, k_ref),
                (v_hbm, v_ref),
                (pos_hbm, pos_ref),
            ]
        )
    ]
    for load in loads:
        load.start()

    h = lax.axis_index("head")
    b = lax.axis_index("blk")
    z = b // 4
    x_hi = (b // 2) % 2
    core = b % 2
    x_lo = h // 4
    y = h % 4
    me = (b % 4) * 8 + h
    right = (h, (b + 4) % 32)
    left = (h, (b + 28) % 32)
    sibling = (h, z * 4 + x_hi * 2 + (1 - core))

    def plane_device(p):
        return (p % 8, z * 4 + p // 8)

    barrier = pltpu.get_barrier_semaphore()

    def greet(i, carry):
        pl.semaphore_signal(
            barrier, inc=1, device_id=plane_device((me + i) % PLANE), device_id_type=MESH
        )
        return carry

    lax.fori_loop(1, PLANE, greet, 0)
    pl.semaphore_signal(barrier, inc=1, device_id=right, device_id_type=MESH)
    pl.semaphore_signal(barrier, inc=1, device_id=left, device_id_type=MESH)

    groups = HQ // LOCAL
    sel_row = lax.broadcasted_iota(jnp.int32, (HQ, groups * D), 0)
    sel_col = lax.broadcasted_iota(jnp.int32, (HQ, groups * D), 1)
    sel_rel = sel_col - ((sel_row // LOCAL) * D + 6 * (sel_row % LOCAL))
    lane32 = lax.broadcasted_iota(jnp.int32, (TOK, HQ), 1)
    delta = jnp.zeros((TOK, HQ), F32)
    for load in loads[:3]:
        load.wait()
    for head in range(HQ):
        cols = slice(head * D, (head + 1) * D)
        term = jnp.sum(
            g_ref[:, cols].astype(F32) * o_ref[:, cols].astype(F32), axis=1, keepdims=True
        )
        delta = jnp.where(lane32 == head, term, delta)
    aux_sum = jnp.zeros((SUB, groups * D), F32)
    parts = pieces_of(lse_ref[...].astype(F32) * (-math.sqrt(D))) + pieces_of(-delta)
    for index, part in enumerate(parts):
        for t in range(2):
            place = jnp.where(sel_rel == 32 * t + index, 1.0, 0.0).astype(BF)
            aux_sum = aux_sum + jnp.dot(
                part[t * SUB : (t + 1) * SUB], place, preferred_element_type=F32
            )
    aux_low = aux_sum.astype(BF)
    for group in range(groups):
        pack_aux[group] = aux_low[:, group * D : (group + 1) * D]
    for load in loads[3:]:
        load.wait()
    for hh in range(2):
        for c in range(2):
            for g in range(4):
                for j in range(2):
                    head = g * 8 + hh * 4 + 2 * c + j
                    cols = slice(head * D, (head + 1) * D)
                    slot = (hh * 2 + c) * 4 + g
                    for t in range(2):
                        rows = slice(t * SUB, (t + 1) * SUB)
                        pack[slot, j, t, 0:SUB, :] = q_ref[rows, cols]
                        pack[slot, j, t, SUB : 2 * SUB, :] = g_ref[rows, cols]

    pl.semaphore_wait(barrier, PLANE + 1)

    key_rows = pl.ds(pl.multiple_of(x_hi * RUN + y * TOK, TOK), TOK)
    my_j = x_hi * 4 + y

    def part_device(j):
        return (x_lo * 4 + j % 4, z * 4 + (j // 4) * 2 + core)

    def kv_copy(i, which):
        j = (my_j + i) % 8
        src = (k_ref, v_ref)[which]
        cols = pl.ds(pl.multiple_of((j % 4) * D, D), D)
        return pltpu.make_async_remote_copy(
            src_ref=src.at[:, cols],
            dst_ref=kv.at[0, which, key_rows, :],
            send_sem=kv_send_sem.at[which, i],
            recv_sem=kv_recv_sem.at[which],
            device_id=part_device(j),
            device_id_type=MESH,
        )

    own_cols = pl.ds(pl.multiple_of(y * D, D), D)
    for which in range(2):

        def kv_start(i, carry, which=which):
            kv_copy(i, which).start()
            return carry

        lax.fori_loop(1, 8, kv_start, 0)
        pltpu.make_async_copy(
            (k_ref, v_ref)[which].at[:, own_cols],
            kv.at[0, which, key_rows, :],
            kv_recv_sem.at[which],
        ).start()

    def q_ends(stage, p):
        slot = (p // 8) * 4 + p % 4
        if stage < 2:
            return pack.at[slot, 0, stage], qd.at[0, stage, me]
        if stage == 2:
            return pack.at[slot, 1], qd.at[2, :, me]
        return pack_aux.at[(p % 4) * 2 + p // 16], aux.at[me]

    def q_copy(stage, i):
        p = (me + i) % PLANE
        src, dst = q_ends(stage, p)
        return pltpu.make_async_remote_copy(
            src_ref=src,
            dst_ref=dst,
            send_sem=q_send_sem.at[stage, i],
            recv_sem=q_recv_sem.at[stage],
            device_id=plane_device(p),
            device_id_type=MESH,
        )

    def q_start(stages):
        def body(i, carry):
            for stage in stages:
                q_copy(stage, i).start()
            return carry

        lax.fori_loop(1, PLANE, body, 0)
        for stage in stages:
            src, dst = q_ends(stage, me)
            pltpu.make_async_copy(src, dst, q_recv_sem.at[stage]).start()

    def all_of(ref, sem):
        pltpu.make_async_copy(ref, ref, sem).wait()

    def ring_copy(src, dst, which, device):
        return pltpu.make_async_remote_copy(
            src_ref=kv.at[src, which],
            dst_ref=kv.at[dst, which],
            send_sem=ring_send_sem.at[which, dst],
            recv_sem=ring_recv_sem.at[which, dst],
            device_id=device,
            device_id_type=MESH,
        )

    def ring_step(i):
        for which in range(2):
            ring_copy(0, 7 - i, which, right).wait_recv()

            @pl.when(i < 3)
            def _(which=which):
                ring_copy(7 - i, 6 - i, which, right).start()
                ring_copy(0, 1 + i, which, left).wait_recv()

            @pl.when(i < 2)
            def _(which=which):
                ring_copy(1 + i, 2 + i, which, left).start()

    q_start((0, 3))
    for which in range(2):
        all_of(kv.at[0, which], kv_recv_sem.at[which])
        ring_copy(0, 7, which, right).start()
        ring_copy(0, 1, which, left).start()
    q_start((1,))
    q_start((2,))

    lane = lax.broadcasted_iota(jnp.int32, (1, HALF), 1)
    run_of = lax.shift_right_logical(lane, 6)
    inside = lax.shift_right_logical(lane, 4) % 4 * TOK + lane % SUB
    run_start = jnp.zeros((1, HALF), jnp.int32)
    for r in range(8):
        run_start = jnp.where(
            run_of == r, pos_ref[z * 4 + r // 2, (r % 2) * RUN], run_start
        )
    for t in range(2):
        qpos[0:1, t * HALF : (t + 1) * HALF] = run_start + inside + t * SUB
    acc[...] = jnp.zeros_like(acc)
    dqt[...] = jnp.zeros_like(dqt)

    aux_row = lax.broadcasted_iota(jnp.int32, (D, HALF), 0)
    ones = jnp.ones((2 * PART, D), BF)

    def local_head(n):
        own = core if n % 2 == 0 else 1 - core
        return 2 * own + n // 2

    def queries_of(n, t, r):
        first = r // SUB
        return qd[n, t, first : first + QT // SUB, 0:SUB, :].reshape(QT, D)

    def cotangents_of(n, t, r):
        first = r // SUB
        return qd[n, t, first : first + QT // SUB, SUB : 2 * SUB, :].reshape(QT, D)

    def prepare(n, t):
        for r in range(0, HALF, QT):
            cols = slice(t * HALF + r, t * HALF + r + QT)
            qt[n, 0:D, cols] = queries_of(n, t, r).T
            gt[n, 0:D, cols] = cotangents_of(n, t, r).T
        first = 32 * t + 6 * local_head(n)
        cols = slice(t * HALF, (t + 1) * HALF)
        every = auxt[...]
        empty = jnp.zeros_like(every)
        qt[n, D : 2 * D, cols] = jnp.where(
            (aux_row >= first) & (aux_row < first + 3), every, empty
        )
        gt[n, D : 2 * D, cols] = jnp.where(
            (aux_row >= first + 3) & (aux_row < first + 6), every, empty
        )

    key_iota = lax.broadcasted_iota(jnp.int32, (RUN, QT), 0)

    def attend(heads, halves, a, c):
        keys = jnp.concatenate([kv[a, 0], kv[c, 0]], axis=0)
        values = jnp.concatenate([kv[a, 1], kv[c, 1]], axis=0)
        keys_wide = jnp.concatenate([keys, ones], axis=1)
        values_wide = jnp.concatenate([values, ones], axis=1)
        keys_t = keys.T
        starts = []
        for j in range(4):
            slot = a if j < 2 else c
            row = ((z + slot) % Z) * 4 + (j % 2) * 2 + core
            starts.append(pos_ref[row, x_lo * RUN])
        dk = jnp.zeros((2 * PART, D), F32)
        dv = jnp.zeros((2 * PART, D), F32)
        for n in heads:
            for t in halves:
                for r in range(0, HALF, QT):
                    cols = slice(t * HALF + r, t * HALF + r + QT)
                    scores = jnp.dot(keys_wide, qt[n, :, cols], preferred_element_type=F32)
                    shifted = jnp.dot(values_wide, gt[n, :, cols], preferred_element_type=F32)
                    raw = jnp.exp2(scores * EXP2_SCALE)
                    where = qpos[0:1, cols]
                    probs = jnp.concatenate(
                        [
                            jnp.where(
                                where - starts[j] >= key_iota, raw[j * RUN : (j + 1) * RUN], 0.0
                            )
                            for j in range(4)
                        ],
                        axis=0,
                    )
                    score_grad = (probs * shifted).astype(BF)
                    dv = dv + jnp.dot(
                        probs.astype(BF), cotangents_of(n, t, r), preferred_element_type=F32
                    )
                    dk = dk + jnp.dot(
                        score_grad, queries_of(n, t, r), preferred_element_type=F32
                    )
                    dqt[n, :, cols] += jnp.dot(
                        keys_t, score_grad, preferred_element_type=F32
                    )
        acc[a, 0] += dk[:PART]
        acc[c, 0] += dk[PART:]
        acc[a, 1] += dv[:PART]
        acc[c, 1] += dv[PART:]

    def slots_of(i):
        return 7 - i, (1 + i) % 4

    def swap(k):
        return pltpu.make_async_remote_copy(
            src_ref=dqx_send.at[k],
            dst_ref=dqx.at[k],
            send_sem=dqx_send_sem.at[k],
            recv_sem=dqx_recv_sem.at[k],
            device_id=sibling,
            device_id_type=MESH,
        )

    def swap_start(k):
        for r in range(0, Q_ROWS, QT):
            dqx_send[k, r : r + QT, :] = (dqt[2 * k + 1, :, r : r + QT] * SCALE).T.astype(BF)
        swap(k).start()

    def dq_columns(k):
        head = y * 8 + x_hi * 4 + 2 * core + k
        return pl.ds(pl.multiple_of(head * D, D), D)

    def dq_copy(k, i):
        p = (me + i) % PLANE
        return pltpu.make_async_remote_copy(
            src_ref=dqs.at[k, :, p],
            dst_ref=dq_recv.at[x_lo, :, :, dq_columns(k)],
            send_sem=dq_send_sem.at[k, i],
            recv_sem=dq_recv_sem,
            device_id=plane_device(p),
            device_id_type=MESH,
        )

    def send_dq(k):
        swap(k).wait_recv()
        for r in range(0, Q_ROWS, QT):
            total = (dqt[2 * k, :, r : r + QT] * SCALE).T + dqx[k, r : r + QT, :].astype(F32)
            first = (r % HALF) // SUB
            dqs[k, r // HALF, first : first + QT // SUB] = total.astype(BF).reshape(
                QT // SUB, SUB, D
            )

        def body(i, carry):
            dq_copy(k, i).start()
            return carry

        lax.fori_loop(1, PLANE, body, 0)
        pltpu.make_async_copy(
            dqs.at[k, :, me], dq_recv.at[x_lo, :, :, dq_columns(k)], dq_recv_sem
        ).start()

    def forward(stage):
        src = qd.at[0, stage] if stage < 2 else qd.at[2]
        dst = qd.at[1, stage] if stage < 2 else qd.at[3]
        return pltpu.make_async_remote_copy(
            src_ref=src,
            dst_ref=dst,
            send_sem=fwd_send_sem.at[stage],
            recv_sem=fwd_recv_sem.at[stage],
            device_id=sibling,
            device_id_type=MESH,
        )

    all_of(qd.at[0, 0], q_recv_sem.at[0])
    forward(0).start()
    all_of(aux, q_recv_sem.at[3])
    auxt[...] = aux[...].reshape(HALF, D).T
    prepare(0, 0)
    ring_step(0)
    forward(0).wait_recv()
    prepare(1, 0)
    attend((0, 1), (0,), 7, 1)
    all_of(qd.at[0, 1], q_recv_sem.at[1])
    forward(1).start()
    prepare(0, 1)
    forward(1).wait_recv()
    prepare(1, 1)
    attend((0, 1), (1,), 7, 1)

    def first_heads(i, carry):
        ring_step(i)
        a, c = slots_of(i)
        attend((0, 1), (0, 1), a, c)
        return carry

    lax.fori_loop(1, 4, first_heads, 0)
    swap_start(0)

    all_of(qd.at[2], q_recv_sem.at[2])
    forward(2).start()
    prepare(2, 0)
    prepare(2, 1)
    send_dq(0)
    forward(2).wait_recv()
    prepare(3, 0)
    prepare(3, 1)

    def rs_copy(src, dst, which, device):
        return pltpu.make_async_remote_copy(
            src_ref=rs_send.at[src, which],
            dst_ref=rs.at[dst, which],
            send_sem=rs_send_sem.at[which, dst],
            recv_sem=rs_recv_sem.at[which, dst],
            device_id=device,
            device_id_type=MESH,
        )

    def last_heads(step, carry):
        a, c = slots_of(3 - step)
        attend((2, 3), (0, 1), a, c)
        down = 4 - step
        up = 4 + step
        for which in range(2):

            @pl.when(step > 0)
            def _(which=which):
                rs_copy(0, down, which, right).wait_recv()
                acc[down, which] += rs[down, which].astype(F32)

            rs_send[down, which] = acc[down, which].astype(BF)
            rs_copy(down, down - 1, which, right).start()

            @pl.when(step > 1)
            def _(which=which):
                rs_copy(0, up, which, left).wait_recv()
                acc[up, which] += rs[up, which].astype(F32)

            @pl.when(step > 0)
            def _(which=which):
                rs_send[up, which] = acc[up, which].astype(BF)
                rs_copy(up, up + 1 - 4 * (up // 7), which, left).start()

        return carry

    lax.fori_loop(0, 4, last_heads, 0)
    swap_start(1)
    send_dq(1)

    def out_copy(i, which):
        j = (my_j + i) % 8
        rows = pl.ds(pl.multiple_of((j // 4) * RUN + (j % 4) * TOK, TOK), TOK)
        return pltpu.make_async_remote_copy(
            src_ref=rs_send.at[0, which, rows, :],
            dst_ref=kv_recv.at[x_hi, which, :, own_cols],
            send_sem=out_send_sem.at[which, i],
            recv_sem=out_recv_sem,
            device_id=part_device(j),
            device_id_type=MESH,
        )

    for which in range(2):
        rs_copy(0, 4, which, left).wait_recv()
        rs_copy(0, 0, which, right).wait_recv()
        rs_send[0, which] = (
            acc[0, which] + rs[4, which].astype(F32) + rs[0, which].astype(F32)
        ).astype(BF)

        def out_start(i, carry, which=which):
            out_copy(i, which).start()
            return carry

        lax.fori_loop(1, 8, out_start, 0)
        pltpu.make_async_copy(
            rs_send.at[0, which, key_rows, :], kv_recv.at[x_hi, which, :, own_cols], out_recv_sem
        ).start()

    all_of(dq_recv, dq_recv_sem)
    for t in range(2):
        for r in range(0, HQ * D, 512):
            cols = slice(r, r + 512)
            total = dq_recv[0, t, :, cols].astype(F32) + dq_recv[1, t, :, cols].astype(F32)
            dq_out[t * SUB : (t + 1) * SUB, cols] = total.astype(BF)
    all_of(kv_recv, out_recv_sem)
    dk_out[...] = ((kv_recv[0, 0].astype(F32) + kv_recv[1, 0].astype(F32)) * SCALE).astype(BF)
    dv_out[...] = (kv_recv[0, 1].astype(F32) + kv_recv[1, 1].astype(F32)).astype(BF)

    def finish_plane(i, carry):
        for stage in range(4):
            q_copy(stage, i).wait_send()
        for k in range(2):
            dq_copy(k, i).wait_send()
        return carry

    lax.fori_loop(1, PLANE, finish_plane, 0)

    def finish_part(i, carry):
        for which in range(2):
            kv_copy(i, which).wait_send()
            out_copy(i, which).wait_send()
        return carry

    lax.fori_loop(1, 8, finish_part, 0)
    for stage in range(3):
        forward(stage).wait_send()
    for k in range(2):
        swap(k).wait_send()
    for which in range(2):
        for dst in range(1, 8):
            ring_copy(0, dst, which, right).wait_send()
        for dst in (0, 1, 2, 3, 4, 6, 7):
            rs_copy(0, dst, which, right).wait_send()


def shards(queries, key_heads, value_heads, outputs, out_grad, log_total, positions):
    vmem = pl.BlockSpec(memory_space=pltpu.VMEM)
    anywhere = pl.BlockSpec(memory_space=pl.ANY)
    dma = pltpu.SemaphoreType.DMA
    return pl.pallas_call(
        kernel,
        out_shape=(
            jax.ShapeDtypeStruct((TOK, HQ * D), BF),
            jax.ShapeDtypeStruct((TOK, KVH * D), BF),
            jax.ShapeDtypeStruct((TOK, KVH * D), BF),
        ),
        in_specs=[anywhere] * 7,
        out_specs=(vmem, vmem, vmem),
        scratch_shapes=[
            pltpu.VMEM((TOK, HQ * D), BF),
            pltpu.VMEM((TOK, KVH * D), BF),
            pltpu.VMEM((TOK, KVH * D), BF),
            pltpu.VMEM((TOK, HQ * D), BF),
            pltpu.VMEM((TOK, HQ * D), BF),
            pltpu.VMEM((TOK, HQ), BF),
            pltpu.SMEM((32, 256), jnp.int32),
            pltpu.VMEM((16, 2, 2, 2 * SUB, D), BF),
            pltpu.VMEM((8, SUB, D), BF),
            pltpu.VMEM((LOCAL, 2, PLANE, 2 * SUB, D), BF),
            pltpu.VMEM((PLANE, SUB, D), BF),
            pltpu.VMEM((D, HALF), BF),
            pltpu.VMEM((LOCAL, 2 * D, Q_ROWS), BF),
            pltpu.VMEM((LOCAL, 2 * D, Q_ROWS), BF),
            pltpu.VMEM((8, Q_ROWS), jnp.int32),
            pltpu.VMEM((Z, 2, PART, D), BF),
            pltpu.VMEM((Z, 2, PART, D), F32),
            pltpu.VMEM((LOCAL, D, Q_ROWS), F32),
            pltpu.VMEM((2, 2, PLANE, SUB, D), BF),
            pltpu.VMEM((2, Q_ROWS, D), BF),
            pltpu.VMEM((2, Q_ROWS, D), BF),
            pltpu.VMEM((Z, 2, PART, D), BF),
            pltpu.VMEM((Z, 2, PART, D), BF),
            pltpu.VMEM((2, 2, SUB, HQ * D), BF),
            pltpu.VMEM((2, 2, TOK, KVH * D), BF),
            dma((7,)),
            dma((4, PLANE)),
            dma((4,)),
            dma((3,)),
            dma((3,)),
            dma((2, 8)),
            dma((2,)),
            dma((2, Z)),
            dma((2, Z)),
            dma((2, Z)),
            dma((2, Z)),
            dma((2,)),
            dma((2,)),
            dma((2, PLANE)),
            dma,
            dma((2, 8)),
            dma,
        ],
        compiler_params=pltpu.CompilerParams(
            collective_id=0, has_side_effects=True, vmem_limit_bytes=60 << 20
        ),
    )(queries, key_heads, value_heads, outputs, out_grad, log_total, positions)


def solution(mesh):
    spec = P(("head", "blk"), None)
    return jax.shard_map(
        shards,
        mesh=mesh,
        in_specs=(spec,) * 6 + (P(),),
        out_specs=(spec,) * 3,
        check_vma=False,
    )
```

```python
import math

import jax
import jax.numpy as jnp
from jax import lax
from jax.experimental import pallas as pl
from jax.experimental.pallas import tpu as pltpu
from jax.sharding import PartitionSpec as P

D = 128
HQ = 32
KVH = 4
TOK = 32
SUB = TOK // 2
PLANE = 32
HALF = PLANE * SUB
PART = 256
RUN = 128
Z = 8
LOCAL = 4
QT = 256
SCALE = 1.0 / math.sqrt(D)
EXP2_SCALE = SCALE * math.log2(math.e)
BF = jnp.bfloat16
F32 = jnp.float32
MESH = pl.DeviceIdType.MESH


def pieces_of(value):
    high = value.astype(BF)
    rest = value - high.astype(F32)
    mid = rest.astype(BF)
    low = (rest - mid.astype(F32)).astype(BF)
    return high, mid, low


def kernel(
    q_hbm,
    k_hbm,
    v_hbm,
    o_hbm,
    g_hbm,
    lse_hbm,
    pos_hbm,
    dq_out,
    dk_out,
    dv_out,
    q_ref,
    k_ref,
    v_ref,
    o_ref,
    g_ref,
    lse_ref,
    pos_ref,
    pack,
    pack_aux,
    qd,
    aux,
    auxt,
    qt,
    gt,
    qpos,
    kv,
    acc,
    dqt,
    dqs,
    dqx_send,
    dqx,
    rs_send,
    rs,
    dq_recv,
    kv_recv,
    in_sem,
    q_send_sem,
    q_recv_sem,
    fwd_send_sem,
    fwd_recv_sem,
    kv_send_sem,
    kv_recv_sem,
    ring_send_sem,
    ring_recv_sem,
    rs_send_sem,
    rs_recv_sem,
    dqx_send_sem,
    dqx_recv_sem,
    dq_send_sem,
    dq_recv_sem,
    out_send_sem,
    out_recv_sem,
):
    loads = [
        pltpu.make_async_copy(src, dst, in_sem.at[index])
        for index, (src, dst) in enumerate(
            [
                (g_hbm, g_ref),
                (o_hbm, o_ref),
                (lse_hbm, lse_ref),
                (q_hbm, q_ref),
                (k_hbm, k_ref),
                (v_hbm, v_ref),
                (pos_hbm, pos_ref),
            ]
        )
    ]
    for load in loads:
        load.start()

    h = lax.axis_index("head")
    b = lax.axis_index("blk")
    z = b // 4
    x_hi = (b // 2) % 2
    core = b % 2
    x_lo = h // 4
    y = h % 4
    me = (b % 4) * 8 + h
    right = (h, (b + 4) % 32)
    left = (h, (b + 28) % 32)
    sibling = (h, z * 4 + x_hi * 2 + (1 - core))

    def plane_device(p):
        return (p % 8, z * 4 + p // 8)

    barrier = pltpu.get_barrier_semaphore()

    def greet(i, carry):
        pl.semaphore_signal(
            barrier, inc=1, device_id=plane_device((me + i) % PLANE), device_id_type=MESH
        )
        return carry

    lax.fori_loop(1, PLANE, greet, 0)
    pl.semaphore_signal(barrier, inc=1, device_id=right, device_id_type=MESH)
    pl.semaphore_signal(barrier, inc=1, device_id=left, device_id_type=MESH)

    groups = HQ // LOCAL
    sel_row = lax.broadcasted_iota(jnp.int32, (HQ, groups * D), 0)
    sel_col = lax.broadcasted_iota(jnp.int32, (HQ, groups * D), 1)
    sel_rel = sel_col - ((sel_row // LOCAL) * D + 6 * (sel_row % LOCAL))
    lane32 = lax.broadcasted_iota(jnp.int32, (TOK, HQ), 1)
    delta = jnp.zeros((TOK, HQ), F32)
    for load in loads[:3]:
        load.wait()
    for head in range(HQ):
        cols = slice(head * D, (head + 1) * D)
        term = jnp.sum(
            g_ref[:, cols].astype(F32) * o_ref[:, cols].astype(F32), axis=1, keepdims=True
        )
        delta = jnp.where(lane32 == head, term, delta)
    aux_sum = jnp.zeros((SUB, groups * D), F32)
    parts = pieces_of(lse_ref[...].astype(F32) * (-math.sqrt(D))) + pieces_of(-delta)
    for index, part in enumerate(parts):
        for t in range(2):
            place = jnp.where(sel_rel == 32 * t + index, 1.0, 0.0).astype(BF)
            aux_sum = aux_sum + jnp.dot(
                part[t * SUB : (t + 1) * SUB], place, preferred_element_type=F32
            )
    aux_low = aux_sum.astype(BF)
    for group in range(groups):
        pack_aux[group] = aux_low[:, group * D : (group + 1) * D]
    for load in loads[3:]:
        load.wait()
    for hh in range(2):
        for c in range(2):
            for g in range(4):
                for j in range(2):
                    head = g * 8 + hh * 4 + 2 * c + j
                    cols = slice(head * D, (head + 1) * D)
                    slot = (hh * 2 + c) * 4 + g
                    for t in range(2):
                        rows = slice(t * SUB, (t + 1) * SUB)
                        pack[slot, j, t, 0:SUB, :] = q_ref[rows, cols]
                        pack[slot, j, t, SUB : 2 * SUB, :] = g_ref[rows, cols]

    pl.semaphore_wait(barrier, PLANE + 1)

    key_rows = pl.ds(pl.multiple_of(x_hi * RUN + y * TOK, TOK), TOK)
    my_j = x_hi * 4 + y

    def part_device(j):
        return (x_lo * 4 + j % 4, z * 4 + (j // 4) * 2 + core)

    def kv_copy(i, which):
        j = (my_j + i) % 8
        src = (k_ref, v_ref)[which]
        cols = pl.ds(pl.multiple_of((j % 4) * D, D), D)
        return pltpu.make_async_remote_copy(
            src_ref=src.at[:, cols],
            dst_ref=kv.at[0, which, key_rows, :],
            send_sem=kv_send_sem.at[which, i],
            recv_sem=kv_recv_sem.at[which],
            device_id=part_device(j),
            device_id_type=MESH,
        )

    own_cols = pl.ds(pl.multiple_of(y * D, D), D)
    for which in range(2):

        def kv_start(i, carry, which=which):
            kv_copy(i, which).start()
            return carry

        lax.fori_loop(1, 8, kv_start, 0)
        pltpu.make_async_copy(
            (k_ref, v_ref)[which].at[:, own_cols],
            kv.at[0, which, key_rows, :],
            kv_recv_sem.at[which],
        ).start()

    def q_ends(stage, p):
        slot = (p // 8) * 4 + p % 4
        if stage < 2:
            return pack.at[slot, 0, stage], qd.at[0, stage, me]
        if stage == 2:
            return pack.at[slot, 1], qd.at[2, :, me]
        return pack_aux.at[(p % 4) * 2 + p // 16], aux.at[me]

    def q_copy(stage, i):
        p = (me + i) % PLANE
        src, dst = q_ends(stage, p)
        return pltpu.make_async_remote_copy(
            src_ref=src,
            dst_ref=dst,
            send_sem=q_send_sem.at[stage, i],
            recv_sem=q_recv_sem.at[stage],
            device_id=plane_device(p),
            device_id_type=MESH,
        )

    def q_start(stages):
        def body(i, carry):
            for stage in stages:
                q_copy(stage, i).start()
            return carry

        lax.fori_loop(1, PLANE, body, 0)
        for stage in stages:
            src, dst = q_ends(stage, me)
            pltpu.make_async_copy(src, dst, q_recv_sem.at[stage]).start()

    def all_of(ref, sem):
        pltpu.make_async_copy(ref, ref, sem).wait()

    def ring_copy(src, dst, which, device):
        return pltpu.make_async_remote_copy(
            src_ref=kv.at[src, which],
            dst_ref=kv.at[dst, which],
            send_sem=ring_send_sem.at[which, dst],
            recv_sem=ring_recv_sem.at[which, dst],
            device_id=device,
            device_id_type=MESH,
        )

    def ring_step(i):
        for which in range(2):
            ring_copy(0, 7 - i, which, right).wait_recv()

            @pl.when(i < 3)
            def _(which=which):
                ring_copy(7 - i, 6 - i, which, right).start()
                ring_copy(0, 1 + i, which, left).wait_recv()

            @pl.when(i < 2)
            def _(which=which):
                ring_copy(1 + i, 2 + i, which, left).start()

    q_start((0, 3))
    for which in range(2):
        all_of(kv.at[0, which], kv_recv_sem.at[which])
        ring_copy(0, 7, which, right).start()
        ring_copy(0, 1, which, left).start()
    q_start((1,))
    q_start((2,))

    lane = lax.broadcasted_iota(jnp.int32, (1, HALF), 1)
    run_of = lax.shift_right_logical(lane, 6)
    inside = lax.shift_right_logical(lane, 4) % 4 * TOK + lane % SUB
    run_start = jnp.zeros((1, HALF), jnp.int32)
    for r in range(8):
        run_start = jnp.where(
            run_of == r, pos_ref[z * 4 + r // 2, (r % 2) * RUN], run_start
        )
    for t in range(2):
        qpos[t, 0:1, :] = run_start + inside + t * SUB
    acc[...] = jnp.zeros_like(acc)
    dqt[...] = jnp.zeros_like(dqt)

    aux_row = lax.broadcasted_iota(jnp.int32, (D, HALF), 0)
    ones = jnp.ones((2 * PART, D), BF)

    def local_head(n):
        return 2 * ((core + n) % 2) + n // 2

    def queries_of(n, t, r):
        first = r // SUB
        return qd[n, t, first : first + QT // SUB, 0:SUB, :].reshape(QT, D)

    def cotangents_of(n, t, r):
        first = r // SUB
        return qd[n, t, first : first + QT // SUB, SUB : 2 * SUB, :].reshape(QT, D)

    def prepare(n, t):
        for r in range(0, HALF, QT):
            cols = slice(r, r + QT)
            qt[n, t, 0:D, cols] = queries_of(n, t, r).T
            gt[n, t, 0:D, cols] = cotangents_of(n, t, r).T
        first = 32 * t + 6 * local_head(n)
        every = auxt[...]
        empty = jnp.zeros_like(every)
        qt[n, t, D : 2 * D, :] = jnp.where(
            (aux_row >= first) & (aux_row < first + 3), every, empty
        )
        gt[n, t, D : 2 * D, :] = jnp.where(
            (aux_row >= first + 3) & (aux_row < first + 6), every, empty
        )

    key_iota = lax.broadcasted_iota(jnp.int32, (RUN, QT), 0)

    def attend(heads, halves, slots):
        keys = jnp.concatenate([kv[slot, 0] for slot in slots], axis=0)
        values = jnp.concatenate([kv[slot, 1] for slot in slots], axis=0)
        keys_wide = jnp.concatenate([keys, ones], axis=1)
        values_wide = jnp.concatenate([values, ones], axis=1)
        keys_t = keys.T
        starts = []
        for slot in slots:
            for half in range(2):
                row = ((z + slot) % Z) * 4 + half * 2 + core
                starts.append(pos_ref[row, x_lo * RUN])
        dk = jnp.zeros((2 * PART, D), F32)
        dv = jnp.zeros((2 * PART, D), F32)
        for n in heads:
            for t in halves:
                for r in range(0, HALF, QT):
                    cols = slice(r, r + QT)
                    scores = jnp.dot(keys_wide, qt[n, t, :, cols], preferred_element_type=F32)
                    shifted = jnp.dot(values_wide, gt[n, t, :, cols], preferred_element_type=F32)
                    raw = jnp.exp2(scores * EXP2_SCALE)
                    where = qpos[t, 0:1, cols]
                    probs = jnp.concatenate(
                        [
                            jnp.where(
                                where - start >= key_iota, raw[m * RUN : (m + 1) * RUN], 0.0
                            )
                            for m, start in enumerate(starts)
                        ],
                        axis=0,
                    )
                    score_grad = (probs * shifted).astype(BF)
                    dv = dv + jnp.dot(
                        probs.astype(BF), cotangents_of(n, t, r), preferred_element_type=F32
                    )
                    dk = dk + jnp.dot(
                        score_grad, queries_of(n, t, r), preferred_element_type=F32
                    )
                    dqt[n, t, :, cols] += jnp.dot(
                        keys_t, score_grad, preferred_element_type=F32
                    )
        for m, slot in enumerate(slots):
            rows = slice(m * PART, (m + 1) * PART)
            acc[slot, 0] += dk[rows]
            acc[slot, 1] += dv[rows]

    def swap(k):
        return pltpu.make_async_remote_copy(
            src_ref=dqx_send.at[k],
            dst_ref=dqx.at[k],
            send_sem=dqx_send_sem.at[k],
            recv_sem=dqx_recv_sem.at[k],
            device_id=sibling,
            device_id_type=MESH,
        )

    def swap_start(k):
        for t in range(2):
            for r in range(0, HALF, QT):
                dqx_send[k, t, r : r + QT, :] = (
                    (dqt[2 * k + 1, t, :, r : r + QT] * SCALE).T.astype(BF)
                )
        swap(k).start()

    def dq_columns(k):
        head = y * 8 + x_hi * 4 + 2 * core + k
        return pl.ds(pl.multiple_of(head * D, D), D)

    def dq_copy(k, i):
        p = (me + i) % PLANE
        return pltpu.make_async_remote_copy(
            src_ref=dqs.at[k, :, p],
            dst_ref=dq_recv.at[x_lo, :, :, dq_columns(k)],
            send_sem=dq_send_sem.at[k, i],
            recv_sem=dq_recv_sem,
            device_id=plane_device(p),
            device_id_type=MESH,
        )

    def send_dq(k):
        swap(k).wait_recv()
        for t in range(2):
            for r in range(0, HALF, QT):
                total = (dqt[2 * k, t, :, r : r + QT] * SCALE).T
                total = total + dqx[k, t, r : r + QT, :].astype(F32)
                first = r // SUB
                dqs[k, t, first : first + QT // SUB] = total.astype(BF).reshape(
                    QT // SUB, SUB, D
                )

        def body(i, carry):
            dq_copy(k, i).start()
            return carry

        lax.fori_loop(1, PLANE, body, 0)
        pltpu.make_async_copy(
            dqs.at[k, :, me], dq_recv.at[x_lo, :, :, dq_columns(k)], dq_recv_sem
        ).start()

    def forward(stage):
        src = qd.at[0, stage] if stage < 2 else qd.at[2]
        dst = qd.at[1, stage] if stage < 2 else qd.at[3]
        return pltpu.make_async_remote_copy(
            src_ref=src,
            dst_ref=dst,
            send_sem=fwd_send_sem.at[stage],
            recv_sem=fwd_recv_sem.at[stage],
            device_id=sibling,
            device_id_type=MESH,
        )

    def rs_copy(src, dst, which, device):
        return pltpu.make_async_remote_copy(
            src_ref=rs_send.at[src, which],
            dst_ref=rs.at[dst, which],
            send_sem=rs_send_sem.at[which, dst],
            recv_sem=rs_recv_sem.at[which, dst],
            device_id=device,
            device_id_type=MESH,
        )

    def reduce_step(slot, first):
        onward, device = (slot - 1, right) if slot < 4 else (slot + 1, left)
        for which in range(2):
            if not first:
                rs_copy(0, slot, which, right).wait_recv()
                acc[slot, which] += rs[slot, which].astype(F32)
            rs_send[slot, which] = acc[slot, which].astype(BF)
            if slot in (1, 7):
                out_start(slot, which)
            else:
                rs_copy(slot, onward, which, device).start()

    out_kinds = {0: 0, 1: 1, 7: 2, 4: 3}

    def out_copy(slot, i, which):
        j = (my_j + i) % 8
        rows = pl.ds(pl.multiple_of((j // 4) * RUN + (j % 4) * TOK, TOK), TOK)
        kind = out_kinds[slot]
        plane = (z + slot) % Z
        return pltpu.make_async_remote_copy(
            src_ref=rs_send.at[slot, which, rows, :],
            dst_ref=kv_recv.at[kind, x_hi, which, :, own_cols],
            send_sem=out_send_sem.at[kind, which, i],
            recv_sem=out_recv_sem,
            device_id=(x_lo * 4 + j % 4, plane * 4 + (j // 4) * 2 + core),
            device_id_type=MESH,
        )

    def out_start(slot, which):
        def body(i, carry):
            out_copy(slot, i, which).start()
            return carry

        lax.fori_loop(1 if slot == 0 else 0, 8, body, 0)
        if slot == 0:
            pltpu.make_async_copy(
                rs_send.at[0, which, key_rows, :],
                kv_recv.at[0, x_hi, which, :, own_cols],
                out_recv_sem,
            ).start()

    def out_direct(slot):
        for which in range(2):
            rs_send[slot, which] = acc[slot, which].astype(BF)
            out_start(slot, which)

    all_of(qd.at[0, 0], q_recv_sem.at[0])
    forward(0).start()
    all_of(aux, q_recv_sem.at[3])
    auxt[...] = aux[...].reshape(HALF, D).T
    prepare(0, 0)

    ring_step(0)
    forward(0).wait_recv()
    prepare(1, 0)
    attend((0, 1), (0,), (7, 1))
    all_of(qd.at[0, 1], q_recv_sem.at[1])
    forward(1).start()
    prepare(0, 1)
    forward(1).wait_recv()
    prepare(1, 1)
    attend((0, 1), (1,), (7, 1))

    steps = ((1, 0), (2, 0), (2, 1), (1, 1), (3, 0), (3, 1))

    def step_of(s, carry):
        pair, head = carry[0] % 4, 2 * (carry[1] % 2)

        @pl.when(s == 0)
        def _():
            ring_step(1)

        @pl.when(s == 1)
        def _():
            ring_step(2)
            all_of(qd.at[2], q_recv_sem.at[2])
            forward(2).start()

        @pl.when(s == 2)
        def _():
            prepare(2, 0)
            prepare(2, 1)
            forward(2).wait_recv()
            prepare(3, 0)
            prepare(3, 1)

        @pl.when(s == 3)
        def _():
            reduce_step(5, True)
            reduce_step(3, True)
            ring_step(3)

        @pl.when(s == 5)
        def _():
            reduce_step(6, False)
            reduce_step(2, False)
            swap_start(0)

        attend((head, head + 1), (0, 1), (7 - pair, (1 + pair) % 4))
        return carry[0] // 4, carry[1] // 2

    lax.fori_loop(
        0,
        len(steps),
        step_of,
        (
            jnp.int32(sum(pair * 4**s for s, (pair, _) in enumerate(steps))),
            jnp.int32(sum(head * 2**s for s, (_, head) in enumerate(steps))),
        ),
    )
    out_direct(4)
    out_direct(0)
    send_dq(0)

    def last(u, carry):
        attend((3 - u,), (0, 1), (7, 1))

        @pl.when(u == 0)
        def _():
            swap_start(1)

        return carry

    lax.fori_loop(0, 2, last, 0)
    reduce_step(1, False)
    reduce_step(7, False)
    send_dq(1)

    all_of(dq_recv, dq_recv_sem)
    for t in range(2):
        for r in range(0, HQ * D, 512):
            cols = slice(r, r + 512)
            total = dq_recv[0, t, :, cols].astype(F32) + dq_recv[1, t, :, cols].astype(F32)
            dq_out[t * SUB : (t + 1) * SUB, cols] = total.astype(BF)
    all_of(kv_recv, out_recv_sem)
    sums = []
    for which in range(2):
        total = jnp.zeros((TOK, KVH * D), F32)
        for kind in range(4):
            for hh in range(2):
                total = total + kv_recv[kind, hh, which].astype(F32)
        sums.append(total)
    dk_out[...] = (sums[0] * SCALE).astype(BF)
    dv_out[...] = sums[1].astype(BF)

    def finish_plane(i, carry):
        for stage in range(4):
            q_copy(stage, i).wait_send()
        for k in range(2):
            dq_copy(k, i).wait_send()
        return carry

    lax.fori_loop(1, PLANE, finish_plane, 0)

    def finish_part(i, carry):
        for which in range(2):
            kv_copy(i, which).wait_send()
            for slot in (0, 1, 7, 4):
                out_copy(slot, i, which).wait_send()
        return carry

    lax.fori_loop(1, 8, finish_part, 0)
    for stage in range(3):
        forward(stage).wait_send()
    for k in range(2):
        swap(k).wait_send()
    for which in range(2):
        for slot in (1, 7, 4):
            out_copy(slot, 0, which).wait_send()
        for dst in range(1, 8):
            ring_copy(0, dst, which, right).wait_send()
        for dst in (1, 2, 6, 7):
            rs_copy(0, dst, which, right).wait_send()


def shards(queries, key_heads, value_heads, outputs, out_grad, log_total, positions):
    vmem = pl.BlockSpec(memory_space=pltpu.VMEM)
    anywhere = pl.BlockSpec(memory_space=pl.ANY)
    dma = pltpu.SemaphoreType.DMA
    return pl.pallas_call(
        kernel,
        out_shape=(
            jax.ShapeDtypeStruct((TOK, HQ * D), BF),
            jax.ShapeDtypeStruct((TOK, KVH * D), BF),
            jax.ShapeDtypeStruct((TOK, KVH * D), BF),
        ),
        in_specs=[anywhere] * 7,
        out_specs=(vmem, vmem, vmem),
        scratch_shapes=[
            pltpu.VMEM((TOK, HQ * D), BF),
            pltpu.VMEM((TOK, KVH * D), BF),
            pltpu.VMEM((TOK, KVH * D), BF),
            pltpu.VMEM((TOK, HQ * D), BF),
            pltpu.VMEM((TOK, HQ * D), BF),
            pltpu.VMEM((TOK, HQ), BF),
            pltpu.SMEM((32, 256), jnp.int32),
            pltpu.VMEM((16, 2, 2, 2 * SUB, D), BF),
            pltpu.VMEM((8, SUB, D), BF),
            pltpu.VMEM((LOCAL, 2, PLANE, 2 * SUB, D), BF),
            pltpu.VMEM((PLANE, SUB, D), BF),
            pltpu.VMEM((D, HALF), BF),
            pltpu.VMEM((LOCAL, 2, 2 * D, HALF), BF),
            pltpu.VMEM((LOCAL, 2, 2 * D, HALF), BF),
            pltpu.VMEM((2, 8, HALF), jnp.int32),
            pltpu.VMEM((Z, 2, PART, D), BF),
            pltpu.VMEM((Z, 2, PART, D), F32),
            pltpu.VMEM((LOCAL, 2, D, HALF), F32),
            pltpu.VMEM((2, 2, PLANE, SUB, D), BF),
            pltpu.VMEM((2, 2, HALF, D), BF),
            pltpu.VMEM((2, 2, HALF, D), BF),
            pltpu.VMEM((Z, 2, PART, D), BF),
            pltpu.VMEM((Z, 2, PART, D), BF),
            pltpu.VMEM((2, 2, SUB, HQ * D), BF),
            pltpu.VMEM((4, 2, 2, TOK, KVH * D), BF),
            dma((7,)),
            dma((4, PLANE)),
            dma((4,)),
            dma((3,)),
            dma((3,)),
            dma((2, 8)),
            dma((2,)),
            dma((2, Z)),
            dma((2, Z)),
            dma((2, Z)),
            dma((2, Z)),
            dma((2,)),
            dma((2,)),
            dma((2, PLANE)),
            dma,
            dma((4, 2, 8)),
            dma,
        ],
        compiler_params=pltpu.CompilerParams(
            collective_id=0, has_side_effects=True, vmem_limit_bytes=60 << 20
        ),
    )(queries, key_heads, value_heads, outputs, out_grad, log_total, positions)


def solution(mesh):
    spec = P(("head", "blk"), None)
    return jax.shard_map(
        shards,
        mesh=mesh,
        in_specs=(spec,) * 6 + (P(),),
        out_specs=(spec,) * 3,
        check_vma=False,
    )
```

```python
import math

import jax
import jax.numpy as jnp
from jax import lax
from jax.experimental import pallas as pl
from jax.experimental.pallas import tpu as pltpu
from jax.sharding import PartitionSpec as P

D = 128
HQ = 32
KVH = 4
TOK = 32
SUB = TOK // 2
PLANE = 32
HALF = PLANE * SUB
PART = 256
RUN = 128
Z = 8
LOCAL = 4
QT = 256
SCALE = 1.0 / math.sqrt(D)
EXP2_SCALE = SCALE * math.log2(math.e)
BF = jnp.bfloat16
F32 = jnp.float32
MESH = pl.DeviceIdType.MESH


def pieces_of(value):
    high = value.astype(BF)
    rest = value - high.astype(F32)
    mid = rest.astype(BF)
    low = (rest - mid.astype(F32)).astype(BF)
    return high, mid, low


def kernel(
    q_hbm,
    k_hbm,
    v_hbm,
    o_hbm,
    g_hbm,
    lse_hbm,
    pos_hbm,
    dq_out,
    dk_out,
    dv_out,
    q_ref,
    k_ref,
    v_ref,
    o_ref,
    g_ref,
    lse_ref,
    pos_ref,
    pack,
    pack_kv,
    qd,
    auxt,
    qt,
    gt,
    qpos,
    kv,
    acc,
    dqt,
    dqs,
    dqx_send,
    dqx,
    rs_send,
    rs,
    dq_recv,
    kv_recv,
    in_sem,
    q_send_sem,
    q_recv_sem,
    fwd_send_sem,
    fwd_recv_sem,
    kv_send_sem,
    kv_recv_sem,
    ring_send_sem,
    ring_recv_sem,
    rs_send_sem,
    rs_recv_sem,
    dqx_send_sem,
    dqx_recv_sem,
    dq_send_sem,
    dq_recv_sem,
    out_send_sem,
    out_recv_sem,
):
    loads = [
        pltpu.make_async_copy(src, dst, in_sem.at[index])
        for index, (src, dst) in enumerate(
            [
                (g_hbm, g_ref),
                (o_hbm, o_ref),
                (lse_hbm, lse_ref),
                (q_hbm, q_ref),
                (k_hbm, k_ref),
                (v_hbm, v_ref),
                (pos_hbm, pos_ref),
            ]
        )
    ]
    for load in loads:
        load.start()

    h = lax.axis_index("head")
    b = lax.axis_index("blk")
    z = b // 4
    x_hi = (b // 2) % 2
    core = b % 2
    x_lo = h // 4
    y = h % 4
    me = (b % 4) * 8 + h
    right = (h, (b + 4) % 32)
    left = (h, (b + 28) % 32)
    sibling = (h, z * 4 + x_hi * 2 + (1 - core))

    def plane_device(p):
        return (p % 8, z * 4 + p // 8)

    barrier = pltpu.get_barrier_semaphore()

    def greet(i, carry):
        pl.semaphore_signal(
            barrier, inc=1, device_id=plane_device((me + i) % PLANE), device_id_type=MESH
        )
        return carry

    lax.fori_loop(1, PLANE, greet, 0)
    pl.semaphore_signal(barrier, inc=1, device_id=right, device_id_type=MESH)
    pl.semaphore_signal(barrier, inc=1, device_id=left, device_id_type=MESH)

    groups = HQ // LOCAL
    sel_row = lax.broadcasted_iota(jnp.int32, (HQ, groups * D), 0)
    sel_col = lax.broadcasted_iota(jnp.int32, (HQ, groups * D), 1)
    sel_rel = sel_col - ((sel_row // LOCAL) * D + 6 * (sel_row % LOCAL))
    lane32 = lax.broadcasted_iota(jnp.int32, (TOK, HQ), 1)
    delta = jnp.zeros((TOK, HQ), F32)
    for load in loads[:3]:
        load.wait()
    for head in range(HQ):
        cols = slice(head * D, (head + 1) * D)
        term = jnp.sum(
            g_ref[:, cols].astype(F32) * o_ref[:, cols].astype(F32), axis=1, keepdims=True
        )
        delta = jnp.where(lane32 == head, term, delta)
    aux_sum = jnp.zeros((SUB, groups * D), F32)
    parts = pieces_of(lse_ref[...].astype(F32) * (-math.sqrt(D))) + pieces_of(-delta)
    for index, part in enumerate(parts):
        for t in range(2):
            place = jnp.where(sel_rel == 32 * t + index, 1.0, 0.0).astype(BF)
            aux_sum = aux_sum + jnp.dot(
                part[t * SUB : (t + 1) * SUB], place, preferred_element_type=F32
            )
    aux_low = aux_sum.astype(BF)
    for load in loads[3:]:
        load.wait()
    for hh in range(2):
        for c in range(2):
            for g in range(4):
                slot = (hh * 2 + c) * 4 + g
                group = g * 2 + hh
                pack[slot, 0, 0, 2 * SUB : 3 * SUB, :] = aux_low[:, group * D : (group + 1) * D]
                for j in range(2):
                    head = g * 8 + hh * 4 + 2 * c + j
                    cols = slice(head * D, (head + 1) * D)
                    for t in range(2):
                        rows = slice(t * SUB, (t + 1) * SUB)
                        pack[slot, j, t, 0:SUB, :] = q_ref[rows, cols]
                        pack[slot, j, t, SUB : 2 * SUB, :] = g_ref[rows, cols]

    for g in range(KVH):
        pack_kv[g, 0] = k_ref[:, g * D : (g + 1) * D]
        pack_kv[g, 1] = v_ref[:, g * D : (g + 1) * D]

    pl.semaphore_wait(barrier, PLANE + 1)

    key_rows = pl.ds(pl.multiple_of(x_hi * RUN + y * TOK, TOK), TOK)
    my_j = x_hi * 4 + y

    def part_device(j):
        return (x_lo * 4 + j % 4, z * 4 + (j // 4) * 2 + core)

    def kv_copy(i):
        j = (my_j + i) % 8
        return pltpu.make_async_remote_copy(
            src_ref=pack_kv.at[j % 4],
            dst_ref=kv.at[0, :, key_rows, :],
            send_sem=kv_send_sem,
            recv_sem=kv_recv_sem,
            device_id=part_device(j),
            device_id_type=MESH,
        )

    own_cols = pl.ds(pl.multiple_of(y * D, D), D)

    def kv_start(i, carry):
        kv_copy(i).start()
        return carry

    lax.fori_loop(1, 8, kv_start, 0)
    pltpu.make_async_copy(pack_kv.at[y], kv.at[0, :, key_rows, :], kv_recv_sem).start()

    def q_ends(stage, p):
        slot = (p // 8) * 4 + p % 4
        if stage == 0:
            return pack.at[slot, 0, 0], qd.at[0, 0, me]
        rows = slice(0, 2 * SUB)
        if stage == 1:
            return pack.at[slot, 0, 1, rows], qd.at[0, 1, me, rows]
        return pack.at[slot, 1, :, rows], qd.at[2, :, me, rows]

    def q_copy(stage, i):
        p = (me + i) % PLANE
        src, dst = q_ends(stage, p)
        return pltpu.make_async_remote_copy(
            src_ref=src,
            dst_ref=dst,
            send_sem=q_send_sem.at[stage],
            recv_sem=q_recv_sem.at[stage],
            device_id=plane_device(p),
            device_id_type=MESH,
        )

    def q_start(stage):
        def body(i, carry):
            q_copy(stage, i).start()
            return carry

        lax.fori_loop(1, PLANE, body, 0)
        src, dst = q_ends(stage, me)
        pltpu.make_async_copy(src, dst, q_recv_sem.at[stage]).start()

    def all_of(ref, sem):
        pltpu.make_async_copy(ref, ref, sem).wait()

    def ring_copy(src, dst, which, device):
        return pltpu.make_async_remote_copy(
            src_ref=kv.at[src, which],
            dst_ref=kv.at[dst, which],
            send_sem=ring_send_sem.at[which, dst],
            recv_sem=ring_recv_sem.at[which, dst],
            device_id=device,
            device_id_type=MESH,
        )

    def ring_step(i):
        for which in range(2):
            ring_copy(0, 7 - i, which, right).wait_recv()

            @pl.when(i < 3)
            def _(which=which):
                ring_copy(7 - i, 6 - i, which, right).start()
                ring_copy(0, 1 + i, which, left).wait_recv()

            @pl.when(i < 2)
            def _(which=which):
                ring_copy(1 + i, 2 + i, which, left).start()

    q_start(0)
    q_start(1)
    all_of(kv.at[0], kv_recv_sem)
    for which in range(2):
        ring_copy(0, 7, which, right).start()
        ring_copy(0, 1, which, left).start()
    q_start(2)

    lane = lax.broadcasted_iota(jnp.int32, (1, HALF), 1)
    run_of = lax.shift_right_logical(lane, 6)
    inside = lax.shift_right_logical(lane, 4) % 4 * TOK + lane % SUB
    run_start = jnp.zeros((1, HALF), jnp.int32)
    for r in range(8):
        run_start = jnp.where(
            run_of == r, pos_ref[z * 4 + r // 2, (r % 2) * RUN], run_start
        )
    for t in range(2):
        qpos[t, 0:1, :] = run_start + inside + t * SUB
    acc[...] = jnp.zeros_like(acc)
    dqt[...] = jnp.zeros_like(dqt)

    aux_row = lax.broadcasted_iota(jnp.int32, (D, HALF), 0)
    ones = jnp.ones((2 * PART, D), BF)

    def local_head(n):
        return 2 * ((core + n) % 2) + n // 2

    def queries_of(n, t, r):
        first = r // SUB
        return qd[n, t, first : first + QT // SUB, 0:SUB, :].reshape(QT, D)

    def cotangents_of(n, t, r):
        first = r // SUB
        return qd[n, t, first : first + QT // SUB, SUB : 2 * SUB, :].reshape(QT, D)

    def prepare(n, t):
        for r in range(0, HALF, QT):
            cols = slice(r, r + QT)
            qt[n, t, 0:D, cols] = queries_of(n, t, r).T
            gt[n, t, 0:D, cols] = cotangents_of(n, t, r).T
        first = 32 * t + 6 * local_head(n)
        every = auxt[...]
        empty = jnp.zeros_like(every)
        qt[n, t, D : 2 * D, :] = jnp.where(
            (aux_row >= first) & (aux_row < first + 3), every, empty
        )
        gt[n, t, D : 2 * D, :] = jnp.where(
            (aux_row >= first + 3) & (aux_row < first + 6), every, empty
        )

    key_iota = lax.broadcasted_iota(jnp.int32, (RUN, QT), 0)

    def attend(heads, halves, slots):
        keys = jnp.concatenate([kv[slot, 0] for slot in slots], axis=0)
        values = jnp.concatenate([kv[slot, 1] for slot in slots], axis=0)
        keys_wide = jnp.concatenate([keys, ones], axis=1)
        values_wide = jnp.concatenate([values, ones], axis=1)
        keys_t = keys.T
        starts = []
        for slot in slots:
            for half in range(2):
                row = ((z + slot) % Z) * 4 + half * 2 + core
                starts.append(pos_ref[row, x_lo * RUN])
        dk = jnp.zeros((2 * PART, D), F32)
        dv = jnp.zeros((2 * PART, D), F32)
        for n in heads:
            for t in halves:
                for r in range(0, HALF, QT):
                    cols = slice(r, r + QT)
                    scores = jnp.dot(keys_wide, qt[n, t, :, cols], preferred_element_type=F32)
                    shifted = jnp.dot(values_wide, gt[n, t, :, cols], preferred_element_type=F32)
                    raw = jnp.exp2(scores * EXP2_SCALE)
                    where = qpos[t, 0:1, cols]
                    probs = jnp.concatenate(
                        [
                            jnp.where(
                                where - start >= key_iota, raw[m * RUN : (m + 1) * RUN], 0.0
                            )
                            for m, start in enumerate(starts)
                        ],
                        axis=0,
                    )
                    score_grad = (probs * shifted).astype(BF)
                    dv = dv + jnp.dot(
                        probs.astype(BF), cotangents_of(n, t, r), preferred_element_type=F32
                    )
                    dk = dk + jnp.dot(
                        score_grad, queries_of(n, t, r), preferred_element_type=F32
                    )
                    dqt[n, t, :, cols] += jnp.dot(
                        keys_t, score_grad, preferred_element_type=F32
                    )
        for m, slot in enumerate(slots):
            rows = slice(m * PART, (m + 1) * PART)
            acc[slot, 0] += dk[rows]
            acc[slot, 1] += dv[rows]

    def swap(k):
        return pltpu.make_async_remote_copy(
            src_ref=dqx_send.at[k],
            dst_ref=dqx.at[k],
            send_sem=dqx_send_sem.at[k],
            recv_sem=dqx_recv_sem.at[k],
            device_id=sibling,
            device_id_type=MESH,
        )

    def swap_start(k):
        for t in range(2):
            for r in range(0, HALF, QT):
                dqx_send[k, t, r : r + QT, :] = (
                    (dqt[2 * k + 1, t, :, r : r + QT] * SCALE).T.astype(BF)
                )
        swap(k).start()

    def dq_columns(k):
        head = y * 8 + x_hi * 4 + 2 * core + k
        return pl.ds(pl.multiple_of(head * D, D), D)

    def dq_copy(k, i):
        p = (me + i) % PLANE
        return pltpu.make_async_remote_copy(
            src_ref=dqs.at[k, :, p],
            dst_ref=dq_recv.at[x_lo, :, :, dq_columns(k)],
            send_sem=dq_send_sem.at[k],
            recv_sem=dq_recv_sem,
            device_id=plane_device(p),
            device_id_type=MESH,
        )

    def send_dq(k):
        swap(k).wait_recv()
        for t in range(2):
            for r in range(0, HALF, QT):
                total = (dqt[2 * k, t, :, r : r + QT] * SCALE).T
                total = total + dqx[k, t, r : r + QT, :].astype(F32)
                first = r // SUB
                dqs[k, t, first : first + QT // SUB] = total.astype(BF).reshape(
                    QT // SUB, SUB, D
                )

        def body(i, carry):
            dq_copy(k, i).start()
            return carry

        lax.fori_loop(1, PLANE, body, 0)
        pltpu.make_async_copy(
            dqs.at[k, :, me], dq_recv.at[x_lo, :, :, dq_columns(k)], dq_recv_sem
        ).start()

    def forward(stage):
        rows = slice(0, 2 * SUB)
        src = qd.at[0, stage, :, rows] if stage < 2 else qd.at[2, :, :, rows]
        dst = qd.at[1, stage, :, rows] if stage < 2 else qd.at[3, :, :, rows]
        return pltpu.make_async_remote_copy(
            src_ref=src,
            dst_ref=dst,
            send_sem=fwd_send_sem.at[stage],
            recv_sem=fwd_recv_sem.at[stage],
            device_id=sibling,
            device_id_type=MESH,
        )

    def rs_copy(src, dst, which, device):
        return pltpu.make_async_remote_copy(
            src_ref=rs_send.at[src, which],
            dst_ref=rs.at[dst, which],
            send_sem=rs_send_sem.at[which, dst],
            recv_sem=rs_recv_sem.at[which, dst],
            device_id=device,
            device_id_type=MESH,
        )

    def reduce_step(slot, first):
        onward, device = (slot - 1, right) if slot < 4 else (slot + 1, left)
        for which in range(2):
            if not first:
                rs_copy(0, slot, which, right).wait_recv()
                acc[slot, which] += rs[slot, which].astype(F32)
            rs_send[slot, which] = acc[slot, which].astype(BF)
            if slot not in (1, 7):
                rs_copy(slot, onward, which, device).start()
        if slot in (1, 7):
            out_start(slot)

    out_kinds = {0: 0, 1: 1, 7: 2, 4: 3}

    def out_copy(slot, i):
        j = (my_j + i) % 8
        rows = pl.ds(pl.multiple_of((j // 4) * RUN + (j % 4) * TOK, TOK), TOK)
        kind = out_kinds[slot]
        plane = (z + slot) % Z
        return pltpu.make_async_remote_copy(
            src_ref=rs_send.at[slot, :, rows, :],
            dst_ref=kv_recv.at[kind, x_hi, :, :, own_cols],
            send_sem=out_send_sem.at[kind],
            recv_sem=out_recv_sem,
            device_id=(x_lo * 4 + j % 4, plane * 4 + (j // 4) * 2 + core),
            device_id_type=MESH,
        )

    def out_start(slot):
        def body(i, carry):
            out_copy(slot, i).start()
            return carry

        lax.fori_loop(1 if slot == 0 else 0, 8, body, 0)
        if slot == 0:
            pltpu.make_async_copy(
                rs_send.at[0, :, key_rows, :],
                kv_recv.at[0, x_hi, :, :, own_cols],
                out_recv_sem,
            ).start()

    def out_direct(slot):
        rs_send[slot] = acc[slot].astype(BF)
        out_start(slot)

    all_of(qd.at[0, 0], q_recv_sem.at[0])
    forward(0).start()
    auxt[...] = qd[0, 0, :, 2 * SUB : 3 * SUB, :].reshape(HALF, D).T
    prepare(0, 0)

    ring_step(0)
    forward(0).wait_recv()
    prepare(1, 0)
    second_half = qd.at[0, 1, :, 0 : 2 * SUB]
    all_of(second_half, q_recv_sem.at[1])
    forward(1).start()
    attend((0, 1), (0,), (7, 1))
    ring_step(1)
    prepare(0, 1)
    forward(1).wait_recv()
    prepare(1, 1)
    attend((0, 1), (1,), (7, 1))

    steps = ((1, 0), (2, 0), (2, 1), (1, 1), (3, 0), (3, 1))

    def step_of(s, carry):
        pair, head = carry[0] % 4, 2 * (carry[1] % 2)

        @pl.when(s == 1)
        def _():
            ring_step(2)
            all_of(qd.at[2, :, :, 0 : 2 * SUB], q_recv_sem.at[2])
            forward(2).start()

        @pl.when(s == 2)
        def _():
            prepare(2, 0)
            prepare(2, 1)
            forward(2).wait_recv()
            prepare(3, 0)
            prepare(3, 1)

        @pl.when(s == 3)
        def _():
            reduce_step(5, True)
            reduce_step(3, True)
            ring_step(3)

        @pl.when(s == 5)
        def _():
            reduce_step(6, False)
            reduce_step(2, False)
            swap_start(0)

        attend((head, head + 1), (0, 1), (7 - pair, (1 + pair) % 4))
        return carry[0] // 4, carry[1] // 2

    lax.fori_loop(
        0,
        len(steps),
        step_of,
        (
            jnp.int32(sum(pair * 4**s for s, (pair, _) in enumerate(steps))),
            jnp.int32(sum(head * 2**s for s, (_, head) in enumerate(steps))),
        ),
    )
    out_direct(4)
    out_direct(0)
    send_dq(0)

    def last(u, carry):
        attend((3 - u,), (0, 1), (7, 1))

        @pl.when(u == 0)
        def _():
            swap_start(1)

        return carry

    lax.fori_loop(0, 2, last, 0)
    reduce_step(1, False)
    reduce_step(7, False)
    send_dq(1)

    all_of(dq_recv, dq_recv_sem)
    for t in range(2):
        for r in range(0, HQ * D, 512):
            cols = slice(r, r + 512)
            total = dq_recv[0, t, :, cols].astype(F32) + dq_recv[1, t, :, cols].astype(F32)
            dq_out[t * SUB : (t + 1) * SUB, cols] = total.astype(BF)
    all_of(kv_recv, out_recv_sem)
    sums = []
    for which in range(2):
        total = jnp.zeros((TOK, KVH * D), F32)
        for kind in range(4):
            for hh in range(2):
                total = total + kv_recv[kind, hh, which].astype(F32)
        sums.append(total)
    dk_out[...] = (sums[0] * SCALE).astype(BF)
    dv_out[...] = sums[1].astype(BF)

    others = PLANE - 1
    all_of(qd.at[0, 0, 0:others], q_send_sem.at[0])
    all_of(qd.at[0, 1, 0:others, 0 : 2 * SUB], q_send_sem.at[1])
    all_of(qd.at[2, :, 0:others, 0 : 2 * SUB], q_send_sem.at[2])
    all_of(kv.at[0, :, 0 : 7 * TOK], kv_send_sem)
    for k in range(2):
        all_of(dqs.at[k, :, 0:others], dq_send_sem.at[k])
        swap(k).wait_send()
    for slot in (1, 7, 4):
        all_of(rs_send.at[slot], out_send_sem.at[out_kinds[slot]])
    all_of(rs_send.at[0, :, 0 : 7 * TOK], out_send_sem.at[0])
    for stage in range(3):
        forward(stage).wait_send()
    for which in range(2):
        for dst in range(1, 8):
            ring_copy(0, dst, which, right).wait_send()
        for dst in (1, 2, 6, 7):
            rs_copy(0, dst, which, right).wait_send()


def shards(queries, key_heads, value_heads, outputs, out_grad, log_total, positions):
    vmem = pl.BlockSpec(memory_space=pltpu.VMEM)
    anywhere = pl.BlockSpec(memory_space=pl.ANY)
    dma = pltpu.SemaphoreType.DMA
    return pl.pallas_call(
        kernel,
        out_shape=(
            jax.ShapeDtypeStruct((TOK, HQ * D), BF),
            jax.ShapeDtypeStruct((TOK, KVH * D), BF),
            jax.ShapeDtypeStruct((TOK, KVH * D), BF),
        ),
        in_specs=[anywhere] * 7,
        out_specs=(vmem, vmem, vmem),
        scratch_shapes=[
            pltpu.VMEM((TOK, HQ * D), BF),
            pltpu.VMEM((TOK, KVH * D), BF),
            pltpu.VMEM((TOK, KVH * D), BF),
            pltpu.VMEM((TOK, HQ * D), BF),
            pltpu.VMEM((TOK, HQ * D), BF),
            pltpu.VMEM((TOK, HQ), BF),
            pltpu.SMEM((32, 256), jnp.int32),
            pltpu.VMEM((16, 2, 2, 3 * SUB, D), BF),
            pltpu.VMEM((KVH, 2, TOK, D), BF),
            pltpu.VMEM((LOCAL, 2, PLANE, 3 * SUB, D), BF),
            pltpu.VMEM((D, HALF), BF),
            pltpu.VMEM((LOCAL, 2, 2 * D, HALF), BF),
            pltpu.VMEM((LOCAL, 2, 2 * D, HALF), BF),
            pltpu.VMEM((2, 8, HALF), jnp.int32),
            pltpu.VMEM((Z, 2, PART, D), BF),
            pltpu.VMEM((Z, 2, PART, D), F32),
            pltpu.VMEM((LOCAL, 2, D, HALF), F32),
            pltpu.VMEM((2, 2, PLANE, SUB, D), BF),
            pltpu.VMEM((2, 2, HALF, D), BF),
            pltpu.VMEM((2, 2, HALF, D), BF),
            pltpu.VMEM((Z, 2, PART, D), BF),
            pltpu.VMEM((Z, 2, PART, D), BF),
            pltpu.VMEM((2, 2, SUB, HQ * D), BF),
            pltpu.VMEM((4, 2, 2, TOK, KVH * D), BF),
            dma((7,)),
            dma((3,)),
            dma((3,)),
            dma((3,)),
            dma((3,)),
            dma,
            dma,
            dma((2, Z)),
            dma((2, Z)),
            dma((2, Z)),
            dma((2, Z)),
            dma((2,)),
            dma((2,)),
            dma((2,)),
            dma,
            dma((4,)),
            dma,
        ],
        compiler_params=pltpu.CompilerParams(
            collective_id=0, has_side_effects=True, vmem_limit_bytes=60 << 20
        ),
    )(queries, key_heads, value_heads, outputs, out_grad, log_total, positions)


def solution(mesh):
    spec = P(("head", "blk"), None)
    return jax.shard_map(
        shards,
        mesh=mesh,
        in_specs=(spec,) * 6 + (P(),),
        out_specs=(spec,) * 3,
        check_vma=False,
    )
```

```python
import math

import jax
import jax.numpy as jnp
from jax import lax
from jax.experimental import pallas as pl
from jax.experimental.pallas import tpu as pltpu
from jax.sharding import PartitionSpec as P

D = 128
HQ = 32
KVH = 4
TOK = 32
SUB = TOK // 2
PLANE = 32
HALF = PLANE * SUB
PART = 256
RUN = 128
Z = 8
LOCAL = 4
QT = 256
SCALE = 1.0 / math.sqrt(D)
EXP2_SCALE = SCALE * math.log2(math.e)
BF = jnp.bfloat16
F32 = jnp.float32
MESH = pl.DeviceIdType.MESH


def pieces_of(value):
    high = value.astype(BF)
    rest = value - high.astype(F32)
    mid = rest.astype(BF)
    low = (rest - mid.astype(F32)).astype(BF)
    return high, mid, low


def kernel(
    q_hbm,
    k_hbm,
    v_hbm,
    o_hbm,
    g_hbm,
    lse_hbm,
    pos_hbm,
    dq_recv,
    kv_recv,
    q_ref,
    k_ref,
    v_ref,
    o_ref,
    g_ref,
    lse_ref,
    pos_ref,
    pack,
    pack_kv,
    qd,
    auxt,
    qt,
    gt,
    qpos,
    kv,
    acc,
    dqt,
    dqs,
    dqx_send,
    dqx,
    rs_send,
    rs,
    in_sem,
    q_send_sem,
    q_recv_sem,
    fwd_send_sem,
    fwd_recv_sem,
    kv_send_sem,
    kv_recv_sem,
    ring_send_sem,
    ring_recv_sem,
    rs_send_sem,
    rs_recv_sem,
    dqx_send_sem,
    dqx_recv_sem,
    dq_send_sem,
    dq_recv_sem,
    out_send_sem,
    out_recv_sem,
):
    loads = [
        pltpu.make_async_copy(src, dst, in_sem.at[index])
        for index, (src, dst) in enumerate(
            [
                (g_hbm, g_ref),
                (o_hbm, o_ref),
                (lse_hbm, lse_ref),
                (q_hbm, q_ref),
                (k_hbm, k_ref),
                (v_hbm, v_ref),
                (pos_hbm, pos_ref),
            ]
        )
    ]
    for load in loads:
        load.start()

    h = lax.axis_index("head")
    b = lax.axis_index("blk")
    z = b // 4
    x_hi = (b // 2) % 2
    core = b % 2
    x_lo = h // 4
    y = h % 4
    me = (b % 4) * 8 + h
    right = (h, (b + 4) % 32)
    left = (h, (b + 28) % 32)
    sibling = (h, z * 4 + x_hi * 2 + (1 - core))

    def plane_device(p):
        return (p % 8, z * 4 + p // 8)

    barrier = pltpu.get_barrier_semaphore()

    def greet(i, carry):
        pl.semaphore_signal(
            barrier, inc=1, device_id=plane_device((me + i) % PLANE), device_id_type=MESH
        )
        return carry

    lax.fori_loop(1, PLANE, greet, 0)
    pl.semaphore_signal(barrier, inc=1, device_id=right, device_id_type=MESH)
    pl.semaphore_signal(barrier, inc=1, device_id=left, device_id_type=MESH)

    groups = HQ // LOCAL
    sel_row = lax.broadcasted_iota(jnp.int32, (HQ, groups * D), 0)
    sel_col = lax.broadcasted_iota(jnp.int32, (HQ, groups * D), 1)
    sel_rel = sel_col - ((sel_row // LOCAL) * D + 6 * (sel_row % LOCAL))
    lane32 = lax.broadcasted_iota(jnp.int32, (TOK, HQ), 1)
    delta = jnp.zeros((TOK, HQ), F32)
    for load in loads[:3]:
        load.wait()
    for head in range(HQ):
        cols = slice(head * D, (head + 1) * D)
        term = jnp.sum(
            g_ref[:, cols].astype(F32) * o_ref[:, cols].astype(F32), axis=1, keepdims=True
        )
        delta = jnp.where(lane32 == head, term, delta)
    aux_sum = jnp.zeros((SUB, groups * D), F32)
    parts = pieces_of(lse_ref[...].astype(F32) * (-math.sqrt(D))) + pieces_of(-delta)
    for index, part in enumerate(parts):
        for t in range(2):
            place = jnp.where(sel_rel == 32 * t + index, 1.0, 0.0).astype(BF)
            aux_sum = aux_sum + jnp.dot(
                part[t * SUB : (t + 1) * SUB], place, preferred_element_type=F32
            )
    aux_low = aux_sum.astype(BF)
    for load in loads[3:]:
        load.wait()
    for hh in range(2):
        for c in range(2):
            for g in range(4):
                slot = (hh * 2 + c) * 4 + g
                group = g * 2 + hh
                pack[slot, 0, 0, 2 * SUB : 3 * SUB, :] = aux_low[:, group * D : (group + 1) * D]
                for j in range(2):
                    head = g * 8 + hh * 4 + 2 * c + j
                    cols = slice(head * D, (head + 1) * D)
                    for t in range(2):
                        rows = slice(t * SUB, (t + 1) * SUB)
                        pack[slot, j, t, 0:SUB, :] = q_ref[rows, cols]
                        pack[slot, j, t, SUB : 2 * SUB, :] = g_ref[rows, cols]

    for g in range(KVH):
        pack_kv[g, 0] = k_ref[:, g * D : (g + 1) * D]
        pack_kv[g, 1] = v_ref[:, g * D : (g + 1) * D]

    pl.semaphore_wait(barrier, PLANE + 1)

    key_rows = pl.ds(pl.multiple_of(x_hi * RUN + y * TOK, TOK), TOK)
    my_j = x_hi * 4 + y

    def part_device(j):
        return (x_lo * 4 + j % 4, z * 4 + (j // 4) * 2 + core)

    def kv_copy(i):
        j = (my_j + i) % 8
        return pltpu.make_async_remote_copy(
            src_ref=pack_kv.at[j % 4],
            dst_ref=kv.at[0, :, key_rows, :],
            send_sem=kv_send_sem,
            recv_sem=kv_recv_sem,
            device_id=part_device(j),
            device_id_type=MESH,
        )

    own_cols = pl.ds(pl.multiple_of(y * D, D), D)

    def kv_start(i, carry):
        kv_copy(i).start()
        return carry

    lax.fori_loop(1, 8, kv_start, 0)
    pltpu.make_async_copy(pack_kv.at[y], kv.at[0, :, key_rows, :], kv_recv_sem).start()

    def q_ends(stage, p):
        slot = (p // 8) * 4 + p % 4
        if stage == 0:
            return pack.at[slot, 0, 0], qd.at[0, 0, me]
        rows = slice(0, 2 * SUB)
        if stage == 1:
            return pack.at[slot, 0, 1, rows], qd.at[0, 1, me, rows]
        return pack.at[slot, 1, :, rows], qd.at[2, :, me, rows]

    def q_copy(stage, i):
        p = (me + i) % PLANE
        src, dst = q_ends(stage, p)
        return pltpu.make_async_remote_copy(
            src_ref=src,
            dst_ref=dst,
            send_sem=q_send_sem.at[stage],
            recv_sem=q_recv_sem.at[stage],
            device_id=plane_device(p),
            device_id_type=MESH,
        )

    def q_start(stage):
        def body(i, carry):
            q_copy(stage, i).start()
            return carry

        lax.fori_loop(1, PLANE, body, 0)
        src, dst = q_ends(stage, me)
        pltpu.make_async_copy(src, dst, q_recv_sem.at[stage]).start()

    def all_of(ref, sem):
        pltpu.make_async_copy(ref, ref, sem).wait()

    def ring_copy(src, dst, which, device):
        return pltpu.make_async_remote_copy(
            src_ref=kv.at[src, which],
            dst_ref=kv.at[dst, which],
            send_sem=ring_send_sem.at[which, dst],
            recv_sem=ring_recv_sem.at[which, dst],
            device_id=device,
            device_id_type=MESH,
        )

    def ring_step(i):
        for which in range(2):
            ring_copy(0, 7 - i, which, right).wait_recv()

            @pl.when(i < 3)
            def _(which=which):
                ring_copy(7 - i, 6 - i, which, right).start()
                ring_copy(0, 1 + i, which, left).wait_recv()

            @pl.when(i < 2)
            def _(which=which):
                ring_copy(1 + i, 2 + i, which, left).start()

    q_start(0)
    q_start(1)
    all_of(kv.at[0], kv_recv_sem)
    for which in range(2):
        ring_copy(0, 7, which, right).start()
        ring_copy(0, 1, which, left).start()
    q_start(2)

    lane = lax.broadcasted_iota(jnp.int32, (1, HALF), 1)
    run_of = lax.shift_right_logical(lane, 6)
    inside = lax.shift_right_logical(lane, 4) % 4 * TOK + lane % SUB
    run_start = jnp.zeros((1, HALF), jnp.int32)
    for r in range(8):
        run_start = jnp.where(
            run_of == r, pos_ref[z * 4 + r // 2, (r % 2) * RUN], run_start
        )
    for t in range(2):
        qpos[t, 0:1, :] = run_start + inside + t * SUB
    acc[...] = jnp.zeros_like(acc)
    dqt[...] = jnp.zeros_like(dqt)

    aux_row = lax.broadcasted_iota(jnp.int32, (D, HALF), 0)
    ones = jnp.ones((2 * PART, D), BF)

    def local_head(n):
        return 2 * ((core + n) % 2) + n // 2

    def queries_of(n, t, r):
        first = r // SUB
        return qd[n, t, first : first + QT // SUB, 0:SUB, :].reshape(QT, D)

    def cotangents_of(n, t, r):
        first = r // SUB
        return qd[n, t, first : first + QT // SUB, SUB : 2 * SUB, :].reshape(QT, D)

    def prepare(n, t):
        for r in range(0, HALF, QT):
            cols = slice(r, r + QT)
            qt[n, t, 0:D, cols] = queries_of(n, t, r).T
            gt[n, t, 0:D, cols] = cotangents_of(n, t, r).T
        first = 32 * t + 6 * local_head(n)
        every = auxt[...]
        empty = jnp.zeros_like(every)
        qt[n, t, D : 2 * D, :] = jnp.where(
            (aux_row >= first) & (aux_row < first + 3), every, empty
        )
        gt[n, t, D : 2 * D, :] = jnp.where(
            (aux_row >= first + 3) & (aux_row < first + 6), every, empty
        )

    key_iota = lax.broadcasted_iota(jnp.int32, (RUN, QT), 0)

    def attend(heads, halves, slots):
        keys = jnp.concatenate([kv[slot, 0] for slot in slots], axis=0)
        values = jnp.concatenate([kv[slot, 1] for slot in slots], axis=0)
        keys_wide = jnp.concatenate([keys, ones], axis=1)
        values_wide = jnp.concatenate([values, ones], axis=1)
        keys_t = keys.T
        starts = []
        for slot in slots:
            for half in range(2):
                row = ((z + slot) % Z) * 4 + half * 2 + core
                starts.append(pos_ref[row, x_lo * RUN])
        dk = jnp.zeros((2 * PART, D), F32)
        dv = jnp.zeros((2 * PART, D), F32)
        for n in heads:
            for t in halves:
                for r in range(0, HALF, QT):
                    cols = slice(r, r + QT)
                    scores = jnp.dot(keys_wide, qt[n, t, :, cols], preferred_element_type=F32)
                    shifted = jnp.dot(values_wide, gt[n, t, :, cols], preferred_element_type=F32)
                    raw = jnp.exp2(scores * EXP2_SCALE)
                    where = qpos[t, 0:1, cols]
                    probs = jnp.concatenate(
                        [
                            jnp.where(
                                where - start >= key_iota, raw[m * RUN : (m + 1) * RUN], 0.0
                            )
                            for m, start in enumerate(starts)
                        ],
                        axis=0,
                    )
                    score_grad = (probs * shifted).astype(BF)
                    dv = dv + jnp.dot(
                        probs.astype(BF), cotangents_of(n, t, r), preferred_element_type=F32
                    )
                    dk = dk + jnp.dot(
                        score_grad, queries_of(n, t, r), preferred_element_type=F32
                    )
                    dqt[n, t, :, cols] += jnp.dot(
                        keys_t, score_grad, preferred_element_type=F32
                    )
        for m, slot in enumerate(slots):
            rows = slice(m * PART, (m + 1) * PART)
            acc[slot, 0] += dk[rows]
            acc[slot, 1] += dv[rows]

    def swap(k):
        return pltpu.make_async_remote_copy(
            src_ref=dqx_send.at[k],
            dst_ref=dqx.at[k],
            send_sem=dqx_send_sem.at[k],
            recv_sem=dqx_recv_sem.at[k],
            device_id=sibling,
            device_id_type=MESH,
        )

    def swap_start(k):
        for t in range(2):
            for r in range(0, HALF, QT):
                dqx_send[k, t, r : r + QT, :] = (
                    (dqt[2 * k + 1, t, :, r : r + QT] * SCALE).T.astype(BF)
                )
        swap(k).start()

    def dq_columns(k):
        head = y * 8 + x_hi * 4 + 2 * core + k
        return pl.ds(pl.multiple_of(head * D, D), D)

    def dq_copy(k, i):
        p = (me + i) % PLANE
        return pltpu.make_async_remote_copy(
            src_ref=dqs.at[k, :, p],
            dst_ref=dq_recv.at[x_lo, :, :, dq_columns(k)],
            send_sem=dq_send_sem.at[k],
            recv_sem=dq_recv_sem,
            device_id=plane_device(p),
            device_id_type=MESH,
        )

    def send_dq(k):
        swap(k).wait_recv()
        for t in range(2):
            for r in range(0, HALF, QT):
                total = (dqt[2 * k, t, :, r : r + QT] * SCALE).T
                total = total + dqx[k, t, r : r + QT, :].astype(F32)
                first = r // SUB
                dqs[k, t, first : first + QT // SUB] = total.astype(BF).reshape(
                    QT // SUB, SUB, D
                )

        def body(i, carry):
            dq_copy(k, i).start()
            return carry

        lax.fori_loop(1, PLANE, body, 0)
        pltpu.make_async_copy(
            dqs.at[k, :, me], dq_recv.at[x_lo, :, :, dq_columns(k)], dq_recv_sem
        ).start()

    def forward(stage):
        rows = slice(0, 2 * SUB)
        src = qd.at[0, stage, :, rows] if stage < 2 else qd.at[2, :, :, rows]
        dst = qd.at[1, stage, :, rows] if stage < 2 else qd.at[3, :, :, rows]
        return pltpu.make_async_remote_copy(
            src_ref=src,
            dst_ref=dst,
            send_sem=fwd_send_sem.at[stage],
            recv_sem=fwd_recv_sem.at[stage],
            device_id=sibling,
            device_id_type=MESH,
        )

    def rs_copy(src, dst, which, device):
        return pltpu.make_async_remote_copy(
            src_ref=rs_send.at[src, which],
            dst_ref=rs.at[dst, which],
            send_sem=rs_send_sem.at[which, dst],
            recv_sem=rs_recv_sem.at[which, dst],
            device_id=device,
            device_id_type=MESH,
        )

    def reduce_step(slot, first):
        onward, device = (slot - 1, right) if slot < 4 else (slot + 1, left)
        for which in range(2):
            if not first:
                rs_copy(0, slot, which, right).wait_recv()
                acc[slot, which] += rs[slot, which].astype(F32)
            rs_send[slot, which] = acc[slot, which].astype(BF)
            if slot not in (1, 7):
                rs_copy(slot, onward, which, device).start()
        if slot in (1, 7):
            out_start(slot)

    out_kinds = {0: 0, 1: 1, 7: 2, 4: 3}

    def out_copy(slot, i):
        j = (my_j + i) % 8
        rows = pl.ds(pl.multiple_of((j // 4) * RUN + (j % 4) * TOK, TOK), TOK)
        kind = out_kinds[slot]
        plane = (z + slot) % Z
        return pltpu.make_async_remote_copy(
            src_ref=rs_send.at[slot, :, rows, :],
            dst_ref=kv_recv.at[kind, x_hi, :, :, own_cols],
            send_sem=out_send_sem.at[kind],
            recv_sem=out_recv_sem,
            device_id=(x_lo * 4 + j % 4, plane * 4 + (j // 4) * 2 + core),
            device_id_type=MESH,
        )

    def out_start(slot):
        def body(i, carry):
            out_copy(slot, i).start()
            return carry

        lax.fori_loop(1 if slot == 0 else 0, 8, body, 0)
        if slot == 0:
            pltpu.make_async_copy(
                rs_send.at[0, :, key_rows, :],
                kv_recv.at[0, x_hi, :, :, own_cols],
                out_recv_sem,
            ).start()

    def out_direct(slot):
        rs_send[slot] = acc[slot].astype(BF)
        out_start(slot)

    ring_step(0)
    all_of(qd.at[0, 0], q_recv_sem.at[0])
    forward(0).start()
    auxt[...] = qd[0, 0, :, 2 * SUB : 3 * SUB, :].reshape(HALF, D).T
    prepare(0, 0)

    def nearest(n, carry):
        @pl.when(n == 1)
        def _():
            forward(0).wait_recv()
            prepare(1, 0)

        attend((n,), (0,), (7, 1))
        return carry

    lax.fori_loop(0, 2, nearest, 0)
    ring_step(1)
    all_of(qd.at[0, 1, :, 0 : 2 * SUB], q_recv_sem.at[1])
    forward(1).start()

    def halves(u, carry):
        t, pair = (u + 1) // 2, (u + 1) % 2

        @pl.when(u == 1)
        def _():
            prepare(0, 1)
            forward(1).wait_recv()
            prepare(1, 1)

        attend((0, 1), (t,), (7 - pair, 1 + pair))
        return carry

    lax.fori_loop(0, 3, halves, 0)

    steps = ((2, 0), (2, 1), (1, 1), (3, 0), (3, 1))

    def step_of(s, carry):
        pair, head = carry[0] % 4, 2 * (carry[1] % 2)

        @pl.when(s == 0)
        def _():
            ring_step(2)
            all_of(qd.at[2, :, :, 0 : 2 * SUB], q_recv_sem.at[2])
            forward(2).start()

        @pl.when(s == 1)
        def _():
            prepare(2, 0)
            prepare(2, 1)
            forward(2).wait_recv()
            prepare(3, 0)
            prepare(3, 1)

        @pl.when(s == 2)
        def _():
            reduce_step(5, True)
            reduce_step(3, True)

        @pl.when(s == 3)
        def _():
            ring_step(3)

        @pl.when(s == 4)
        def _():
            reduce_step(6, False)
            reduce_step(2, False)
            swap_start(0)

        attend((head, head + 1), (0, 1), (7 - pair, (1 + pair) % 4))
        return carry[0] // 4, carry[1] // 2

    lax.fori_loop(
        0,
        len(steps),
        step_of,
        (
            jnp.int32(sum(pair * 4**s for s, (pair, _) in enumerate(steps))),
            jnp.int32(sum(head * 2**s for s, (_, head) in enumerate(steps))),
        ),
    )
    out_direct(4)
    out_direct(0)
    send_dq(0)

    def last(u, carry):
        attend((3 - u,), (0, 1), (7, 1))

        @pl.when(u == 0)
        def _():
            swap_start(1)

        return carry

    lax.fori_loop(0, 2, last, 0)
    reduce_step(1, False)
    reduce_step(7, False)
    send_dq(1)

    all_of(dq_recv, dq_recv_sem)
    all_of(kv_recv, out_recv_sem)

    others = PLANE - 1
    all_of(qd.at[0, 0, 0:others], q_send_sem.at[0])
    all_of(qd.at[0, 1, 0:others, 0 : 2 * SUB], q_send_sem.at[1])
    all_of(qd.at[2, :, 0:others, 0 : 2 * SUB], q_send_sem.at[2])
    all_of(kv.at[0, :, 0 : 7 * TOK], kv_send_sem)
    for k in range(2):
        all_of(dqs.at[k, :, 0:others], dq_send_sem.at[k])
        swap(k).wait_send()
    for slot in (1, 7, 4):
        all_of(rs_send.at[slot], out_send_sem.at[out_kinds[slot]])
    all_of(rs_send.at[0, :, 0 : 7 * TOK], out_send_sem.at[0])
    for stage in range(3):
        forward(stage).wait_send()
    for which in range(2):
        for dst in range(1, 8):
            ring_copy(0, dst, which, right).wait_send()
        for dst in (1, 2, 6, 7):
            rs_copy(0, dst, which, right).wait_send()


def owner_sums(dq_parts, kv_parts, dq_out, dk_out, dv_out):
    for t in range(2):
        for r in range(0, HQ * D, 512):
            cols = slice(r, r + 512)
            total = dq_parts[0, t, :, cols].astype(F32) + dq_parts[1, t, :, cols].astype(F32)
            dq_out[t * SUB : (t + 1) * SUB, cols] = total.astype(BF)
    sums = []
    for which in range(2):
        total = jnp.zeros((TOK, KVH * D), F32)
        for kind in range(4):
            for hh in range(2):
                total = total + kv_parts[kind, hh, which].astype(F32)
        sums.append(total)
    dk_out[...] = (sums[0] * SCALE).astype(BF)
    dv_out[...] = sums[1].astype(BF)


def shards(queries, key_heads, value_heads, outputs, out_grad, log_total, positions):
    vmem = pl.BlockSpec(memory_space=pltpu.VMEM)
    anywhere = pl.BlockSpec(memory_space=pl.ANY)
    dma = pltpu.SemaphoreType.DMA
    parts = pl.pallas_call(
        kernel,
        out_shape=(
            jax.ShapeDtypeStruct((2, 2, SUB, HQ * D), BF),
            jax.ShapeDtypeStruct((4, 2, 2, TOK, KVH * D), BF),
        ),
        in_specs=[anywhere] * 7,
        out_specs=(anywhere, anywhere),
        scratch_shapes=[
            pltpu.VMEM((TOK, HQ * D), BF),
            pltpu.VMEM((TOK, KVH * D), BF),
            pltpu.VMEM((TOK, KVH * D), BF),
            pltpu.VMEM((TOK, HQ * D), BF),
            pltpu.VMEM((TOK, HQ * D), BF),
            pltpu.VMEM((TOK, HQ), BF),
            pltpu.SMEM((32, 256), jnp.int32),
            pltpu.VMEM((16, 2, 2, 3 * SUB, D), BF),
            pltpu.VMEM((KVH, 2, TOK, D), BF),
            pltpu.VMEM((LOCAL, 2, PLANE, 3 * SUB, D), BF),
            pltpu.VMEM((D, HALF), BF),
            pltpu.VMEM((LOCAL, 2, 2 * D, HALF), BF),
            pltpu.VMEM((LOCAL, 2, 2 * D, HALF), BF),
            pltpu.VMEM((2, 8, HALF), jnp.int32),
            pltpu.VMEM((Z, 2, PART, D), BF),
            pltpu.VMEM((Z, 2, PART, D), F32),
            pltpu.VMEM((LOCAL, 2, D, HALF), F32),
            pltpu.VMEM((2, 2, PLANE, SUB, D), BF),
            pltpu.VMEM((2, 2, HALF, D), BF),
            pltpu.VMEM((2, 2, HALF, D), BF),
            pltpu.VMEM((Z, 2, PART, D), BF),
            pltpu.VMEM((Z, 2, PART, D), BF),
            dma((7,)),
            dma((3,)),
            dma((3,)),
            dma((3,)),
            dma((3,)),
            dma,
            dma,
            dma((2, Z)),
            dma((2, Z)),
            dma((2, Z)),
            dma((2, Z)),
            dma((2,)),
            dma((2,)),
            dma((2,)),
            dma,
            dma((4,)),
            dma,
        ],
        compiler_params=pltpu.CompilerParams(
            collective_id=0, has_side_effects=True, vmem_limit_bytes=60 << 20
        ),
    )(queries, key_heads, value_heads, outputs, out_grad, log_total, positions)
    return pl.pallas_call(
        owner_sums,
        out_shape=(
            jax.ShapeDtypeStruct((TOK, HQ * D), BF),
            jax.ShapeDtypeStruct((TOK, KVH * D), BF),
            jax.ShapeDtypeStruct((TOK, KVH * D), BF),
        ),
        in_specs=[vmem, vmem],
        out_specs=(vmem, vmem, vmem),
    )(*parts)


def solution(mesh):
    spec = P(("head", "blk"), None)
    return jax.shard_map(
        shards,
        mesh=mesh,
        in_specs=(spec,) * 6 + (P(),),
        out_specs=(spec,) * 3,
        check_vma=False,
    )
```

```python
import math

import jax
import jax.numpy as jnp
from jax import lax
from jax.experimental import pallas as pl
from jax.experimental.pallas import tpu as pltpu
from jax.sharding import PartitionSpec as P

D = 128
HQ = 32
KVH = 4
TOK = 32
SUB = TOK // 2
PLANE = 32
HALF = PLANE * SUB
PART = 256
RUN = 128
Z = 8
LOCAL = 4
QT = 256
SCALE = 1.0 / math.sqrt(D)
EXP2_SCALE = SCALE * math.log2(math.e)
BF = jnp.bfloat16
F32 = jnp.float32
MESH = pl.DeviceIdType.MESH


def pieces_of(value):
    high = value.astype(BF)
    rest = value - high.astype(F32)
    mid = rest.astype(BF)
    low = (rest - mid.astype(F32)).astype(BF)
    return high, mid, low


def kernel(
    q_hbm,
    k_hbm,
    v_hbm,
    o_hbm,
    g_hbm,
    lse_hbm,
    pos_hbm,
    dq_recv,
    kv_recv,
    q_ref,
    k_ref,
    v_ref,
    o_ref,
    g_ref,
    lse_ref,
    pos_ref,
    pack,
    pack_kv,
    qd,
    auxt,
    qt,
    gt,
    qpos,
    kv,
    acc,
    dqt,
    dqs,
    dqx_send,
    dqx,
    rs_send,
    rs,
    in_sem,
    q_send_sem,
    q_recv_sem,
    fwd_send_sem,
    fwd_recv_sem,
    kv_send_sem,
    kv_recv_sem,
    ring_send_sem,
    ring_recv_sem,
    rs_send_sem,
    rs_recv_sem,
    dqx_send_sem,
    dqx_recv_sem,
    dq_send_sem,
    dq_recv_sem,
    out_send_sem,
    out_recv_sem,
):
    loads = [
        pltpu.make_async_copy(src, dst, in_sem.at[index])
        for index, (src, dst) in enumerate(
            [
                (g_hbm, g_ref),
                (o_hbm, o_ref),
                (lse_hbm, lse_ref),
                (q_hbm, q_ref),
                (k_hbm, k_ref),
                (v_hbm, v_ref),
                (pos_hbm, pos_ref),
            ]
        )
    ]
    for load in loads:
        load.start()

    h = lax.axis_index("head")
    b = lax.axis_index("blk")
    z = b // 4
    x_hi = (b // 2) % 2
    core = b % 2
    x_lo = h // 4
    y = h % 4
    me = (b % 4) * 8 + h
    right = (h, (b + 4) % 32)
    left = (h, (b + 28) % 32)
    sibling = (h, z * 4 + x_hi * 2 + (1 - core))

    def plane_device(p):
        return (p % 8, z * 4 + p // 8)

    barrier = pltpu.get_barrier_semaphore()

    def greet(i, carry):
        pl.semaphore_signal(
            barrier, inc=1, device_id=plane_device((me + i) % PLANE), device_id_type=MESH
        )
        return carry

    lax.fori_loop(1, PLANE, greet, 0)
    pl.semaphore_signal(barrier, inc=1, device_id=right, device_id_type=MESH)
    pl.semaphore_signal(barrier, inc=1, device_id=left, device_id_type=MESH)

    groups = HQ // LOCAL
    sel_row = lax.broadcasted_iota(jnp.int32, (HQ, groups * D), 0)
    sel_col = lax.broadcasted_iota(jnp.int32, (HQ, groups * D), 1)
    sel_rel = sel_col - ((sel_row // LOCAL) * D + 6 * (sel_row % LOCAL))
    lane32 = lax.broadcasted_iota(jnp.int32, (TOK, HQ), 1)
    delta = jnp.zeros((TOK, HQ), F32)
    for load in loads[:3]:
        load.wait()
    for head in range(HQ):
        cols = slice(head * D, (head + 1) * D)
        term = jnp.sum(
            g_ref[:, cols].astype(F32) * o_ref[:, cols].astype(F32), axis=1, keepdims=True
        )
        delta = jnp.where(lane32 == head, term, delta)
    aux_sum = jnp.zeros((SUB, groups * D), F32)
    parts = pieces_of(lse_ref[...].astype(F32) * (-math.sqrt(D))) + pieces_of(-delta)
    for index, part in enumerate(parts):
        for t in range(2):
            place = jnp.where(sel_rel == 32 * t + index, 1.0, 0.0).astype(BF)
            aux_sum = aux_sum + jnp.dot(
                part[t * SUB : (t + 1) * SUB], place, preferred_element_type=F32
            )
    aux_low = aux_sum.astype(BF)
    for load in loads[3:]:
        load.wait()
    for hh in range(2):
        for c in range(2):
            for g in range(4):
                slot = (hh * 2 + c) * 4 + g
                group = g * 2 + hh
                pack[slot, 0, 0, 2 * SUB : 3 * SUB, :] = aux_low[:, group * D : (group + 1) * D]
                for j in range(2):
                    head = g * 8 + hh * 4 + 2 * c + j
                    cols = slice(head * D, (head + 1) * D)
                    for t in range(2):
                        rows = slice(t * SUB, (t + 1) * SUB)
                        pack[slot, j, t, 0:SUB, :] = q_ref[rows, cols]
                        pack[slot, j, t, SUB : 2 * SUB, :] = g_ref[rows, cols]

    for g in range(KVH):
        pack_kv[g, 0] = k_ref[:, g * D : (g + 1) * D]
        pack_kv[g, 1] = v_ref[:, g * D : (g + 1) * D]

    pl.semaphore_wait(barrier, PLANE + 1)

    key_rows = pl.ds(pl.multiple_of(x_hi * RUN + y * TOK, TOK), TOK)
    my_j = x_hi * 4 + y

    def part_device(j):
        return (x_lo * 4 + j % 4, z * 4 + (j // 4) * 2 + core)

    def kv_copy(i):
        j = (my_j + i) % 8
        return pltpu.make_async_remote_copy(
            src_ref=pack_kv.at[j % 4],
            dst_ref=kv.at[0, :, key_rows, :],
            send_sem=kv_send_sem,
            recv_sem=kv_recv_sem,
            device_id=part_device(j),
            device_id_type=MESH,
        )

    own_cols = pl.ds(pl.multiple_of(y * D, D), D)

    def kv_start(i, carry):
        kv_copy(i).start()
        return carry

    lax.fori_loop(1, 8, kv_start, 0)
    pltpu.make_async_copy(pack_kv.at[y], kv.at[0, :, key_rows, :], kv_recv_sem).start()

    def q_ends(stage, p):
        slot = (p // 8) * 4 + p % 4
        if stage == 0:
            return pack.at[slot, 0, 0], qd.at[0, 0, me]
        rows = slice(0, 2 * SUB)
        if stage == 1:
            return pack.at[slot, 0, 1, rows], qd.at[0, 1, me, rows]
        return pack.at[slot, 1, :, rows], qd.at[2, :, me, rows]

    def q_copy(stage, i):
        p = (me + i) % PLANE
        src, dst = q_ends(stage, p)
        return pltpu.make_async_remote_copy(
            src_ref=src,
            dst_ref=dst,
            send_sem=q_send_sem.at[stage],
            recv_sem=q_recv_sem.at[stage],
            device_id=plane_device(p),
            device_id_type=MESH,
        )

    def q_start(stage):
        def body(i, carry):
            q_copy(stage, i).start()
            return carry

        lax.fori_loop(1, PLANE, body, 0)
        src, dst = q_ends(stage, me)
        pltpu.make_async_copy(src, dst, q_recv_sem.at[stage]).start()

    def all_of(ref, sem):
        pltpu.make_async_copy(ref, ref, sem).wait()

    def ring_copy(src, dst, which, device):
        return pltpu.make_async_remote_copy(
            src_ref=kv.at[src, which],
            dst_ref=kv.at[dst, which],
            send_sem=ring_send_sem.at[which, dst],
            recv_sem=ring_recv_sem.at[which, dst],
            device_id=device,
            device_id_type=MESH,
        )

    def ring_step(i):
        for which in range(2):
            ring_copy(0, 7 - i, which, right).wait_recv()

            @pl.when(i < 3)
            def _(which=which):
                ring_copy(7 - i, 6 - i, which, right).start()
                ring_copy(0, 1 + i, which, left).wait_recv()

            @pl.when(i < 2)
            def _(which=which):
                ring_copy(1 + i, 2 + i, which, left).start()

    q_start(0)
    q_start(1)
    all_of(kv.at[0], kv_recv_sem)
    for which in range(2):
        ring_copy(0, 7, which, right).start()
        ring_copy(0, 1, which, left).start()
    q_start(2)

    lane = lax.broadcasted_iota(jnp.int32, (1, HALF), 1)
    run_of = lax.shift_right_logical(lane, 6)
    inside = lax.shift_right_logical(lane, 4) % 4 * TOK + lane % SUB
    run_start = jnp.zeros((1, HALF), jnp.int32)
    for r in range(8):
        run_start = jnp.where(
            run_of == r, pos_ref[z * 4 + r // 2, (r % 2) * RUN], run_start
        )
    for t in range(2):
        qpos[t, 0:1, :] = run_start + inside + t * SUB
    acc[...] = jnp.zeros_like(acc)
    dqt[...] = jnp.zeros_like(dqt)

    aux_row = lax.broadcasted_iota(jnp.int32, (D, HALF), 0)
    ones = jnp.ones((2 * PART, D), BF)

    def local_head(n):
        return 2 * ((core + n) % 2) + n // 2

    def queries_of(n, t, r):
        first = r // SUB
        return qd[n, t, first : first + QT // SUB, 0:SUB, :].reshape(QT, D)

    def cotangents_of(n, t, r):
        first = r // SUB
        return qd[n, t, first : first + QT // SUB, SUB : 2 * SUB, :].reshape(QT, D)

    def prepare(n, t):
        for r in range(0, HALF, QT):
            cols = slice(r, r + QT)
            qt[n, t, 0:D, cols] = queries_of(n, t, r).T
            gt[n, t, 0:D, cols] = cotangents_of(n, t, r).T
        first = 32 * t + 6 * local_head(n)
        every = auxt[...]
        empty = jnp.zeros_like(every)
        qt[n, t, D : 2 * D, :] = jnp.where(
            (aux_row >= first) & (aux_row < first + 3), every, empty
        )
        gt[n, t, D : 2 * D, :] = jnp.where(
            (aux_row >= first + 3) & (aux_row < first + 6), every, empty
        )

    key_iota = lax.broadcasted_iota(jnp.int32, (RUN, QT), 0)

    def attend(heads, halves, slots):
        keys = jnp.concatenate([kv[slot, 0] for slot in slots], axis=0)
        values = jnp.concatenate([kv[slot, 1] for slot in slots], axis=0)
        keys_wide = jnp.concatenate([keys, ones], axis=1)
        values_wide = jnp.concatenate([values, ones], axis=1)
        keys_t = keys.T
        starts = []
        for slot in slots:
            for half in range(2):
                row = ((z + slot) % Z) * 4 + half * 2 + core
                starts.append(pos_ref[row, x_lo * RUN])
        dk = jnp.zeros((2 * PART, D), F32)
        dv = jnp.zeros((2 * PART, D), F32)
        for n in heads:
            for t in halves:
                for r in range(0, HALF, QT):
                    cols = slice(r, r + QT)
                    scores = jnp.dot(keys_wide, qt[n, t, :, cols], preferred_element_type=F32)
                    shifted = jnp.dot(values_wide, gt[n, t, :, cols], preferred_element_type=F32)
                    raw = jnp.exp2(scores * EXP2_SCALE)
                    where = qpos[t, 0:1, cols]
                    probs = jnp.concatenate(
                        [
                            jnp.where(
                                where - start >= key_iota, raw[m * RUN : (m + 1) * RUN], 0.0
                            )
                            for m, start in enumerate(starts)
                        ],
                        axis=0,
                    )
                    score_grad = (probs * shifted).astype(BF)
                    dv = dv + jnp.dot(
                        probs.astype(BF), cotangents_of(n, t, r), preferred_element_type=F32
                    )
                    dk = dk + jnp.dot(
                        score_grad, queries_of(n, t, r), preferred_element_type=F32
                    )
                    dqt[n, t, :, cols] += jnp.dot(
                        keys_t, score_grad, preferred_element_type=F32
                    )
        for m, slot in enumerate(slots):
            rows = slice(m * PART, (m + 1) * PART)
            acc[slot, 0] += dk[rows]
            acc[slot, 1] += dv[rows]

    def swap(k):
        return pltpu.make_async_remote_copy(
            src_ref=dqx_send.at[k],
            dst_ref=dqx.at[k],
            send_sem=dqx_send_sem.at[k],
            recv_sem=dqx_recv_sem.at[k],
            device_id=sibling,
            device_id_type=MESH,
        )

    def swap_start(k):
        for t in range(2):
            dqx_send[k, t] = (dqt[2 * k + 1, t] * SCALE).astype(BF)
        swap(k).start()

    def dq_columns(k):
        head = y * 8 + x_hi * 4 + 2 * core + k
        return pl.ds(pl.multiple_of(head * D, D), D)

    def dq_copy(k, i):
        p = (me + i) % PLANE
        return pltpu.make_async_remote_copy(
            src_ref=dqs.at[k, :, p],
            dst_ref=dq_recv.at[x_lo, :, :, dq_columns(k)],
            send_sem=dq_send_sem.at[k],
            recv_sem=dq_recv_sem,
            device_id=plane_device(p),
            device_id_type=MESH,
        )

    def send_dq(k):
        swap(k).wait_recv()
        for t in range(2):
            for r in range(0, HALF, QT):
                cols = slice(r, r + QT)
                total = dqt[2 * k, t, :, cols] * SCALE + dqx[k, t, :, cols].astype(F32)
                first = r // SUB
                dqs[k, t, first : first + QT // SUB] = total.astype(BF).T.reshape(
                    QT // SUB, SUB, D
                )

        def body(i, carry):
            dq_copy(k, i).start()
            return carry

        lax.fori_loop(1, PLANE, body, 0)
        pltpu.make_async_copy(
            dqs.at[k, :, me], dq_recv.at[x_lo, :, :, dq_columns(k)], dq_recv_sem
        ).start()

    def forward(stage):
        rows = slice(0, 2 * SUB)
        src = qd.at[0, stage, :, rows] if stage < 2 else qd.at[2, :, :, rows]
        dst = qd.at[1, stage, :, rows] if stage < 2 else qd.at[3, :, :, rows]
        return pltpu.make_async_remote_copy(
            src_ref=src,
            dst_ref=dst,
            send_sem=fwd_send_sem.at[stage],
            recv_sem=fwd_recv_sem.at[stage],
            device_id=sibling,
            device_id_type=MESH,
        )

    def rs_copy(src, dst, which, device):
        return pltpu.make_async_remote_copy(
            src_ref=rs_send.at[src, which],
            dst_ref=rs.at[dst, which],
            send_sem=rs_send_sem.at[which, dst],
            recv_sem=rs_recv_sem.at[which, dst],
            device_id=device,
            device_id_type=MESH,
        )

    def reduce_step(slot, first):
        onward, device = (slot - 1, right) if slot < 4 else (slot + 1, left)
        for which in range(2):
            if not first:
                rs_copy(0, slot, which, right).wait_recv()
                acc[slot, which] += rs[slot, which].astype(F32)
            rs_send[slot, which] = acc[slot, which].astype(BF)
            if slot not in (1, 7):
                rs_copy(slot, onward, which, device).start()
        if slot in (1, 7):
            out_start(slot)

    out_kinds = {0: 0, 1: 1, 7: 2, 4: 3}

    def out_copy(slot, i):
        j = (my_j + i) % 8
        rows = pl.ds(pl.multiple_of((j // 4) * RUN + (j % 4) * TOK, TOK), TOK)
        kind = out_kinds[slot]
        plane = (z + slot) % Z
        return pltpu.make_async_remote_copy(
            src_ref=rs_send.at[slot, :, rows, :],
            dst_ref=kv_recv.at[kind, x_hi, :, :, own_cols],
            send_sem=out_send_sem.at[kind],
            recv_sem=out_recv_sem,
            device_id=(x_lo * 4 + j % 4, plane * 4 + (j // 4) * 2 + core),
            device_id_type=MESH,
        )

    def out_start(slot):
        def body(i, carry):
            out_copy(slot, i).start()
            return carry

        lax.fori_loop(1 if slot == 0 else 0, 8, body, 0)
        if slot == 0:
            pltpu.make_async_copy(
                rs_send.at[0, :, key_rows, :],
                kv_recv.at[0, x_hi, :, :, own_cols],
                out_recv_sem,
            ).start()

    def out_direct(slot):
        rs_send[slot] = acc[slot].astype(BF)
        out_start(slot)

    ring_step(0)
    all_of(qd.at[0, 0], q_recv_sem.at[0])
    forward(0).start()
    auxt[...] = qd[0, 0, :, 2 * SUB : 3 * SUB, :].reshape(HALF, D).T
    prepare(0, 0)

    def nearest(n, carry):
        @pl.when(n == 1)
        def _():
            forward(0).wait_recv()
            prepare(1, 0)

        attend((n,), (0,), (7, 1))
        return carry

    lax.fori_loop(0, 2, nearest, 0)
    ring_step(1)
    all_of(qd.at[0, 1, :, 0 : 2 * SUB], q_recv_sem.at[1])
    forward(1).start()

    def halves(u, carry):
        t, pair = (u + 1) // 2, (u + 1) % 2

        @pl.when(u == 1)
        def _():
            prepare(0, 1)
            forward(1).wait_recv()
            prepare(1, 1)

        attend((0, 1), (t,), (7 - pair, 1 + pair))
        return carry

    lax.fori_loop(0, 3, halves, 0)

    steps = ((2, 0), (2, 1), (3, 0), (3, 1), (1, 1))

    def step_of(s, carry):
        pair, head = carry[0] % 4, 2 * (carry[1] % 2)

        @pl.when(s == 0)
        def _():
            ring_step(2)
            all_of(qd.at[2, :, :, 0 : 2 * SUB], q_recv_sem.at[2])
            forward(2).start()

        @pl.when(s == 1)
        def _():
            prepare(2, 0)
            prepare(2, 1)
            forward(2).wait_recv()
            prepare(3, 0)
            prepare(3, 1)

        @pl.when(s == 2)
        def _():
            reduce_step(5, True)
            reduce_step(3, True)
            ring_step(3)

        @pl.when(s == 3)
        def _():
            swap_start(0)

        @pl.when(s == 4)
        def _():
            out_direct(4)
            out_direct(0)
            send_dq(0)

        attend((head, head + 1), (0, 1), (7 - pair, (1 + pair) % 4))
        return carry[0] // 4, carry[1] // 2

    lax.fori_loop(
        0,
        len(steps),
        step_of,
        (
            jnp.int32(sum(pair * 4**s for s, (pair, _) in enumerate(steps))),
            jnp.int32(sum(head * 2**s for s, (_, head) in enumerate(steps))),
        ),
    )
    reduce_step(6, False)
    reduce_step(2, False)

    def last(u, carry):
        attend((3 - u,), (0, 1), (7, 1))

        @pl.when(u == 0)
        def _():
            swap_start(1)

        return carry

    lax.fori_loop(0, 2, last, 0)
    send_dq(1)
    reduce_step(1, False)
    reduce_step(7, False)

    all_of(dq_recv, dq_recv_sem)
    all_of(kv_recv, out_recv_sem)

    others = PLANE - 1
    all_of(qd.at[0, 0, 0:others], q_send_sem.at[0])
    all_of(qd.at[0, 1, 0:others, 0 : 2 * SUB], q_send_sem.at[1])
    all_of(qd.at[2, :, 0:others, 0 : 2 * SUB], q_send_sem.at[2])
    all_of(kv.at[0, :, 0 : 7 * TOK], kv_send_sem)
    for k in range(2):
        all_of(dqs.at[k, :, 0:others], dq_send_sem.at[k])
        swap(k).wait_send()
    for slot in (1, 7, 4):
        all_of(rs_send.at[slot], out_send_sem.at[out_kinds[slot]])
    all_of(rs_send.at[0, :, 0 : 7 * TOK], out_send_sem.at[0])
    for stage in range(3):
        forward(stage).wait_send()
    for which in range(2):
        for dst in range(1, 8):
            ring_copy(0, dst, which, right).wait_send()
        for dst in (1, 2, 6, 7):
            rs_copy(0, dst, which, right).wait_send()


def owner_sums(dq_parts, kv_parts, dq_out, dk_out, dv_out):
    for t in range(2):
        for r in range(0, HQ * D, 512):
            cols = slice(r, r + 512)
            total = dq_parts[0, t, :, cols].astype(F32) + dq_parts[1, t, :, cols].astype(F32)
            dq_out[t * SUB : (t + 1) * SUB, cols] = total.astype(BF)
    sums = []
    for which in range(2):
        total = jnp.zeros((TOK, KVH * D), F32)
        for kind in range(4):
            for hh in range(2):
                total = total + kv_parts[kind, hh, which].astype(F32)
        sums.append(total)
    dk_out[...] = (sums[0] * SCALE).astype(BF)
    dv_out[...] = sums[1].astype(BF)


def shards(queries, key_heads, value_heads, outputs, out_grad, log_total, positions):
    vmem = pl.BlockSpec(memory_space=pltpu.VMEM)
    anywhere = pl.BlockSpec(memory_space=pl.ANY)
    dma = pltpu.SemaphoreType.DMA
    parts = pl.pallas_call(
        kernel,
        out_shape=(
            jax.ShapeDtypeStruct((2, 2, SUB, HQ * D), BF),
            jax.ShapeDtypeStruct((4, 2, 2, TOK, KVH * D), BF),
        ),
        in_specs=[anywhere] * 7,
        out_specs=(anywhere, anywhere),
        scratch_shapes=[
            pltpu.VMEM((TOK, HQ * D), BF),
            pltpu.VMEM((TOK, KVH * D), BF),
            pltpu.VMEM((TOK, KVH * D), BF),
            pltpu.VMEM((TOK, HQ * D), BF),
            pltpu.VMEM((TOK, HQ * D), BF),
            pltpu.VMEM((TOK, HQ), BF),
            pltpu.SMEM((32, 256), jnp.int32),
            pltpu.VMEM((16, 2, 2, 3 * SUB, D), BF),
            pltpu.VMEM((KVH, 2, TOK, D), BF),
            pltpu.VMEM((LOCAL, 2, PLANE, 3 * SUB, D), BF),
            pltpu.VMEM((D, HALF), BF),
            pltpu.VMEM((LOCAL, 2, 2 * D, HALF), BF),
            pltpu.VMEM((LOCAL, 2, 2 * D, HALF), BF),
            pltpu.VMEM((2, 8, HALF), jnp.int32),
            pltpu.VMEM((Z, 2, PART, D), BF),
            pltpu.VMEM((Z, 2, PART, D), F32),
            pltpu.VMEM((LOCAL, 2, D, HALF), F32),
            pltpu.VMEM((2, 2, PLANE, SUB, D), BF),
            pltpu.VMEM((2, 2, D, HALF), BF),
            pltpu.VMEM((2, 2, D, HALF), BF),
            pltpu.VMEM((Z, 2, PART, D), BF),
            pltpu.VMEM((Z, 2, PART, D), BF),
            dma((7,)),
            dma((3,)),
            dma((3,)),
            dma((3,)),
            dma((3,)),
            dma,
            dma,
            dma((2, Z)),
            dma((2, Z)),
            dma((2, Z)),
            dma((2, Z)),
            dma((2,)),
            dma((2,)),
            dma((2,)),
            dma,
            dma((4,)),
            dma,
        ],
        compiler_params=pltpu.CompilerParams(
            collective_id=0, has_side_effects=True, vmem_limit_bytes=60 << 20
        ),
    )(queries, key_heads, value_heads, outputs, out_grad, log_total, positions)
    return pl.pallas_call(
        owner_sums,
        out_shape=(
            jax.ShapeDtypeStruct((TOK, HQ * D), BF),
            jax.ShapeDtypeStruct((TOK, KVH * D), BF),
            jax.ShapeDtypeStruct((TOK, KVH * D), BF),
        ),
        in_specs=[vmem, vmem],
        out_specs=(vmem, vmem, vmem),
    )(*parts)


def solution(mesh):
    spec = P(("head", "blk"), None)
    return jax.shard_map(
        shards,
        mesh=mesh,
        in_specs=(spec,) * 6 + (P(),),
        out_specs=(spec,) * 3,
        check_vma=False,
    )
```

```python
import math

import jax
import jax.numpy as jnp
from jax import lax
from jax.experimental import pallas as pl
from jax.experimental.pallas import tpu as pltpu
from jax.sharding import PartitionSpec as P

D = 128
HQ = 32
KVH = 4
TOK = 32
SUB = TOK // 2
PLANE = 32
HALF = PLANE * SUB
PART = 256
RUN = 128
Z = 8
LOCAL = 4
QT = 256
SCALE = 1.0 / math.sqrt(D)
EXP2_SCALE = SCALE * math.log2(math.e)
BF = jnp.bfloat16
F32 = jnp.float32
MESH = pl.DeviceIdType.MESH


def pieces_of(value):
    high = value.astype(BF)
    rest = value - high.astype(F32)
    mid = rest.astype(BF)
    low = (rest - mid.astype(F32)).astype(BF)
    return high, mid, low


def kernel(
    q_hbm,
    k_hbm,
    v_hbm,
    o_hbm,
    g_hbm,
    lse_hbm,
    pos_hbm,
    dq_recv,
    kv_recv,
    q_ref,
    k_ref,
    v_ref,
    o_ref,
    g_ref,
    lse_ref,
    pos_ref,
    pack,
    pack_kv,
    qd,
    auxt,
    qt,
    gt,
    qpos,
    kv,
    acc,
    dqt,
    dqs,
    dqx_send,
    dqx,
    rs_send,
    rs,
    in_sem,
    q_send_sem,
    q_recv_sem,
    fwd_send_sem,
    fwd_recv_sem,
    kv_send_sem,
    kv_recv_sem,
    ring_send_sem,
    ring_recv_sem,
    rs_send_sem,
    rs_recv_sem,
    dqx_send_sem,
    dqx_recv_sem,
    dq_send_sem,
    dq_recv_sem,
    out_send_sem,
    out_recv_sem,
):
    loads = [
        pltpu.make_async_copy(src, dst, in_sem.at[index])
        for index, (src, dst) in enumerate(
            [
                (g_hbm, g_ref),
                (o_hbm, o_ref),
                (lse_hbm, lse_ref),
                (q_hbm, q_ref),
                (k_hbm, k_ref),
                (v_hbm, v_ref),
                (pos_hbm, pos_ref),
            ]
        )
    ]
    for load in loads:
        load.start()

    h = lax.axis_index("head")
    b = lax.axis_index("blk")
    z = b // 4
    x_hi = (b // 2) % 2
    core = b % 2
    x_lo = h // 4
    y = h % 4
    me = (b % 4) * 8 + h
    right = (h, (b + 4) % 32)
    left = (h, (b + 28) % 32)
    sibling = (h, z * 4 + x_hi * 2 + (1 - core))

    def plane_device(p):
        return (p % 8, z * 4 + p // 8)

    barrier = pltpu.get_barrier_semaphore()

    def greet(i, carry):
        pl.semaphore_signal(
            barrier, inc=1, device_id=plane_device((me + i) % PLANE), device_id_type=MESH
        )
        return carry

    lax.fori_loop(1, PLANE, greet, 0)
    pl.semaphore_signal(barrier, inc=1, device_id=right, device_id_type=MESH)
    pl.semaphore_signal(barrier, inc=1, device_id=left, device_id_type=MESH)

    groups = HQ // LOCAL
    sel_row = lax.broadcasted_iota(jnp.int32, (HQ, groups * D), 0)
    sel_col = lax.broadcasted_iota(jnp.int32, (HQ, groups * D), 1)
    sel_rel = sel_col - ((sel_row // LOCAL) * D + 6 * (sel_row % LOCAL))
    lane32 = lax.broadcasted_iota(jnp.int32, (TOK, HQ), 1)
    delta = jnp.zeros((TOK, HQ), F32)
    for load in loads[:3]:
        load.wait()
    for head in range(HQ):
        cols = slice(head * D, (head + 1) * D)
        term = jnp.sum(
            g_ref[:, cols].astype(F32) * o_ref[:, cols].astype(F32), axis=1, keepdims=True
        )
        delta = jnp.where(lane32 == head, term, delta)
    aux_sum = jnp.zeros((SUB, groups * D), F32)
    parts = pieces_of(lse_ref[...].astype(F32) * (-math.sqrt(D))) + pieces_of(-delta)
    for index, part in enumerate(parts):
        for t in range(2):
            place = jnp.where(sel_rel == 32 * t + index, 1.0, 0.0).astype(BF)
            aux_sum = aux_sum + jnp.dot(
                part[t * SUB : (t + 1) * SUB], place, preferred_element_type=F32
            )
    aux_low = aux_sum.astype(BF)
    for load in loads[3:]:
        load.wait()
    for hh in range(2):
        for c in range(2):
            for g in range(4):
                slot = (hh * 2 + c) * 4 + g
                group = g * 2 + hh
                pack[slot, 0, 0, 2 * SUB : 3 * SUB, :] = aux_low[:, group * D : (group + 1) * D]
                for j in range(2):
                    head = g * 8 + hh * 4 + 2 * c + j
                    cols = slice(head * D, (head + 1) * D)
                    for t in range(2):
                        rows = slice(t * SUB, (t + 1) * SUB)
                        pack[slot, j, t, 0:SUB, :] = q_ref[rows, cols]
                        pack[slot, j, t, SUB : 2 * SUB, :] = g_ref[rows, cols]

    for g in range(KVH):
        pack_kv[g, 0] = k_ref[:, g * D : (g + 1) * D]
        pack_kv[g, 1] = v_ref[:, g * D : (g + 1) * D]

    pl.semaphore_wait(barrier, PLANE + 1)

    key_rows = pl.ds(pl.multiple_of(x_hi * RUN + y * TOK, TOK), TOK)
    my_j = x_hi * 4 + y

    def part_device(j):
        return (x_lo * 4 + j % 4, z * 4 + (j // 4) * 2 + core)

    def kv_copy(i):
        j = (my_j + i) % 8
        return pltpu.make_async_remote_copy(
            src_ref=pack_kv.at[j % 4],
            dst_ref=kv.at[0, :, key_rows, :],
            send_sem=kv_send_sem,
            recv_sem=kv_recv_sem,
            device_id=part_device(j),
            device_id_type=MESH,
        )

    own_cols = pl.ds(pl.multiple_of(y * D, D), D)

    def kv_start(i, carry):
        kv_copy(i).start()
        return carry

    lax.fori_loop(1, 8, kv_start, 0)
    pltpu.make_async_copy(pack_kv.at[y], kv.at[0, :, key_rows, :], kv_recv_sem).start()

    def q_ends(stage, p):
        slot = (p // 8) * 4 + p % 4
        if stage == 0:
            return pack.at[slot, 0, 0], qd.at[0, 0, me]
        rows = slice(0, 2 * SUB)
        if stage == 1:
            return pack.at[slot, 0, 1, rows], qd.at[0, 1, me, rows]
        return pack.at[slot, 1, :, rows], qd.at[2, :, me, rows]

    def q_copy(stage, i):
        p = (me + i) % PLANE
        src, dst = q_ends(stage, p)
        return pltpu.make_async_remote_copy(
            src_ref=src,
            dst_ref=dst,
            send_sem=q_send_sem.at[stage],
            recv_sem=q_recv_sem.at[stage],
            device_id=plane_device(p),
            device_id_type=MESH,
        )

    def q_start(stage):
        def body(i, carry):
            q_copy(stage, i).start()
            return carry

        lax.fori_loop(1, PLANE, body, 0)
        src, dst = q_ends(stage, me)
        pltpu.make_async_copy(src, dst, q_recv_sem.at[stage]).start()

    def all_of(ref, sem):
        pltpu.make_async_copy(ref, ref, sem).wait()

    def ring_copy(src, dst, which, device):
        return pltpu.make_async_remote_copy(
            src_ref=kv.at[src, which],
            dst_ref=kv.at[dst, which],
            send_sem=ring_send_sem.at[which],
            recv_sem=ring_recv_sem.at[which, dst],
            device_id=device,
            device_id_type=MESH,
        )

    def ring_step(i):
        for which in range(2):
            ring_copy(0, 7 - i, which, right).wait_recv()

            @pl.when(i < 3)
            def _(which=which):
                ring_copy(7 - i, 6 - i, which, right).start()
                ring_copy(0, 1 + i, which, left).wait_recv()

            @pl.when(i < 2)
            def _(which=which):
                ring_copy(1 + i, 2 + i, which, left).start()

    q_start(0)
    q_start(1)
    all_of(kv.at[0], kv_recv_sem)
    for which in range(2):
        ring_copy(0, 7, which, right).start()
        ring_copy(0, 1, which, left).start()
    q_start(2)

    lane = lax.broadcasted_iota(jnp.int32, (1, HALF), 1)
    run_of = lax.shift_right_logical(lane, 6)
    inside = lax.shift_right_logical(lane, 4) % 4 * TOK + lane % SUB
    run_start = jnp.zeros((1, HALF), jnp.int32)
    for r in range(8):
        run_start = jnp.where(
            run_of == r, pos_ref[z * 4 + r // 2, (r % 2) * RUN], run_start
        )
    for t in range(2):
        qpos[t, 0:1, :] = run_start + inside + t * SUB
    acc[...] = jnp.zeros_like(acc)
    dqt[...] = jnp.zeros_like(dqt)

    aux_row = lax.broadcasted_iota(jnp.int32, (D, HALF), 0)
    ones = jnp.ones((2 * PART, D), BF)

    def local_head(n):
        return 2 * ((core + n) % 2) + n // 2

    def queries_of(n, t, r):
        first = r // SUB
        return qd[n, t, first : first + QT // SUB, 0:SUB, :].reshape(QT, D)

    def cotangents_of(n, t, r):
        first = r // SUB
        return qd[n, t, first : first + QT // SUB, SUB : 2 * SUB, :].reshape(QT, D)

    def prepare(n, t):
        for r in range(0, HALF, QT):
            cols = slice(r, r + QT)
            qt[n, t, 0:D, cols] = queries_of(n, t, r).T
            gt[n, t, 0:D, cols] = cotangents_of(n, t, r).T
        first = 32 * t + 6 * local_head(n)
        every = auxt[...]
        empty = jnp.zeros_like(every)
        qt[n, t, D : 2 * D, :] = jnp.where(
            (aux_row >= first) & (aux_row < first + 3), every, empty
        )
        gt[n, t, D : 2 * D, :] = jnp.where(
            (aux_row >= first + 3) & (aux_row < first + 6), every, empty
        )

    key_iota = lax.broadcasted_iota(jnp.int32, (RUN, QT), 0)

    def attend(heads, halves, slots):
        keys = jnp.concatenate([kv[slot, 0] for slot in slots], axis=0)
        values = jnp.concatenate([kv[slot, 1] for slot in slots], axis=0)
        keys_wide = jnp.concatenate([keys, ones], axis=1)
        values_wide = jnp.concatenate([values, ones], axis=1)
        keys_t = keys.T
        starts = []
        for slot in slots:
            for half in range(2):
                row = ((z + slot) % Z) * 4 + half * 2 + core
                starts.append(pos_ref[row, x_lo * RUN])
        dk = jnp.zeros((2 * PART, D), F32)
        dv = jnp.zeros((2 * PART, D), F32)
        for n in heads:
            for t in halves:
                for r in range(0, HALF, QT):
                    cols = slice(r, r + QT)
                    scores = jnp.dot(keys_wide, qt[n, t, :, cols], preferred_element_type=F32)
                    shifted = jnp.dot(values_wide, gt[n, t, :, cols], preferred_element_type=F32)
                    raw = jnp.exp2(scores * EXP2_SCALE)
                    where = qpos[t, 0:1, cols]
                    probs = jnp.concatenate(
                        [
                            jnp.where(
                                where - start >= key_iota, raw[m * RUN : (m + 1) * RUN], 0.0
                            )
                            for m, start in enumerate(starts)
                        ],
                        axis=0,
                    )
                    score_grad = (probs * shifted).astype(BF)
                    dv = dv + jnp.dot(
                        probs.astype(BF), cotangents_of(n, t, r), preferred_element_type=F32
                    )
                    dk = dk + jnp.dot(
                        score_grad, queries_of(n, t, r), preferred_element_type=F32
                    )
                    dqt[n, t, :, cols] += jnp.dot(
                        keys_t, score_grad, preferred_element_type=F32
                    )
        for m, slot in enumerate(slots):
            rows = slice(m * PART, (m + 1) * PART)
            acc[slot, 0] += dk[rows]
            acc[slot, 1] += dv[rows]

    def swap(k):
        return pltpu.make_async_remote_copy(
            src_ref=dqx_send.at[k],
            dst_ref=dqx.at[k],
            send_sem=dqx_send_sem.at[k],
            recv_sem=dqx_recv_sem.at[k],
            device_id=sibling,
            device_id_type=MESH,
        )

    def swap_start(k):
        for t in range(2):
            dqx_send[k, t] = (dqt[2 * k + 1, t] * SCALE).astype(BF)
        swap(k).start()

    def dq_columns(k):
        head = y * 8 + x_hi * 4 + 2 * core + k
        return pl.ds(pl.multiple_of(head * D, D), D)

    def dq_copy(k, i):
        p = (me + i) % PLANE
        return pltpu.make_async_remote_copy(
            src_ref=dqs.at[k, :, p],
            dst_ref=dq_recv.at[x_lo, :, :, dq_columns(k)],
            send_sem=dq_send_sem.at[k],
            recv_sem=dq_recv_sem,
            device_id=plane_device(p),
            device_id_type=MESH,
        )

    def send_dq(k):
        swap(k).wait_recv()
        for t in range(2):
            for r in range(0, HALF, QT):
                cols = slice(r, r + QT)
                total = dqt[2 * k, t, :, cols] * SCALE + dqx[k, t, :, cols].astype(F32)
                first = r // SUB
                dqs[k, t, first : first + QT // SUB] = total.astype(BF).T.reshape(
                    QT // SUB, SUB, D
                )

        def body(i, carry):
            dq_copy(k, i).start()
            return carry

        lax.fori_loop(1, PLANE, body, 0)
        pltpu.make_async_copy(
            dqs.at[k, :, me], dq_recv.at[x_lo, :, :, dq_columns(k)], dq_recv_sem
        ).start()

    def forward(stage):
        rows = slice(0, 2 * SUB)
        src = qd.at[0, stage, :, rows] if stage < 2 else qd.at[2, :, :, rows]
        dst = qd.at[1, stage, :, rows] if stage < 2 else qd.at[3, :, :, rows]
        return pltpu.make_async_remote_copy(
            src_ref=src,
            dst_ref=dst,
            send_sem=fwd_send_sem.at[stage],
            recv_sem=fwd_recv_sem.at[stage],
            device_id=sibling,
            device_id_type=MESH,
        )

    def rs_copy(src, dst, which, device):
        return pltpu.make_async_remote_copy(
            src_ref=rs_send.at[src, which],
            dst_ref=rs.at[dst, which],
            send_sem=rs_send_sem.at[which],
            recv_sem=rs_recv_sem.at[which, dst],
            device_id=device,
            device_id_type=MESH,
        )

    def reduce_step(slot, first):
        onward, device = (slot - 1, right) if slot < 4 else (slot + 1, left)
        for which in range(2):
            if not first:
                rs_copy(0, slot, which, right).wait_recv()
                acc[slot, which] += rs[slot, which].astype(F32)
            rs_send[slot, which] = acc[slot, which].astype(BF)
            if slot not in (1, 7):
                rs_copy(slot, onward, which, device).start()
        if slot in (1, 7):
            out_start(slot)

    out_kinds = {0: 0, 1: 1, 7: 2, 4: 3}

    def out_copy(slot, i):
        j = (my_j + i) % 8
        rows = pl.ds(pl.multiple_of((j // 4) * RUN + (j % 4) * TOK, TOK), TOK)
        kind = out_kinds[slot]
        plane = (z + slot) % Z
        return pltpu.make_async_remote_copy(
            src_ref=rs_send.at[slot, :, rows, :],
            dst_ref=kv_recv.at[kind, x_hi, :, :, own_cols],
            send_sem=out_send_sem.at[kind],
            recv_sem=out_recv_sem,
            device_id=(x_lo * 4 + j % 4, plane * 4 + (j // 4) * 2 + core),
            device_id_type=MESH,
        )

    def out_start(slot):
        def body(i, carry):
            out_copy(slot, i).start()
            return carry

        lax.fori_loop(1 if slot == 0 else 0, 8, body, 0)
        if slot == 0:
            pltpu.make_async_copy(
                rs_send.at[0, :, key_rows, :],
                kv_recv.at[0, x_hi, :, :, own_cols],
                out_recv_sem,
            ).start()

    def out_direct(slot):
        rs_send[slot] = acc[slot].astype(BF)
        out_start(slot)

    ring_step(0)
    all_of(qd.at[0, 0], q_recv_sem.at[0])
    forward(0).start()
    auxt[...] = qd[0, 0, :, 2 * SUB : 3 * SUB, :].reshape(HALF, D).T
    prepare(0, 0)

    def nearest(n, carry):
        @pl.when(n == 1)
        def _():
            forward(0).wait_recv()
            prepare(1, 0)

        attend((n,), (0,), (7, 1))
        return carry

    lax.fori_loop(0, 2, nearest, 0)
    ring_step(1)
    all_of(qd.at[0, 1, :, 0 : 2 * SUB], q_recv_sem.at[1])
    forward(1).start()

    def halves(u, carry):
        t, pair = (u + 1) // 2, (u + 1) % 2

        @pl.when(u == 1)
        def _():
            prepare(0, 1)
            forward(1).wait_recv()
            prepare(1, 1)

        attend((0, 1), (t,), (7 - pair, 1 + pair))
        return carry

    lax.fori_loop(0, 3, halves, 0)

    steps = ((2, 0), (2, 1), (3, 0), (3, 1), (1, 1))

    def step_of(s, carry):
        pair, head = carry[0] % 4, 2 * (carry[1] % 2)

        @pl.when(s == 0)
        def _():
            ring_step(2)
            all_of(qd.at[2, :, :, 0 : 2 * SUB], q_recv_sem.at[2])
            forward(2).start()

        @pl.when(s == 1)
        def _():
            prepare(2, 0)
            prepare(2, 1)
            forward(2).wait_recv()
            prepare(3, 0)
            prepare(3, 1)

        @pl.when(s == 2)
        def _():
            reduce_step(5, True)
            reduce_step(3, True)
            ring_step(3)

        @pl.when(s == 3)
        def _():
            swap_start(0)

        @pl.when(s == 4)
        def _():
            out_direct(4)
            out_direct(0)
            send_dq(0)

        attend((head, head + 1), (0, 1), (7 - pair, (1 + pair) % 4))
        return carry[0] // 4, carry[1] // 2

    lax.fori_loop(
        0,
        len(steps),
        step_of,
        (
            jnp.int32(sum(pair * 4**s for s, (pair, _) in enumerate(steps))),
            jnp.int32(sum(head * 2**s for s, (_, head) in enumerate(steps))),
        ),
    )
    reduce_step(6, False)
    reduce_step(2, False)

    def last(u, carry):
        attend((3 - u,), (0, 1), (7, 1))

        @pl.when(u == 0)
        def _():
            swap_start(1)

        return carry

    lax.fori_loop(0, 2, last, 0)
    send_dq(1)
    reduce_step(1, False)
    reduce_step(7, False)

    all_of(dq_recv, dq_recv_sem)
    all_of(kv_recv, out_recv_sem)

    others = PLANE - 1
    all_of(qd.at[0, 0, 0:others], q_send_sem.at[0])
    all_of(qd.at[0, 1, 0:others, 0 : 2 * SUB], q_send_sem.at[1])
    all_of(qd.at[2, :, 0:others, 0 : 2 * SUB], q_send_sem.at[2])
    all_of(kv.at[0, :, 0 : 7 * TOK], kv_send_sem)
    for k in range(2):
        all_of(dqs.at[k, :, 0:others], dq_send_sem.at[k])
        swap(k).wait_send()
    for slot in (1, 7, 4):
        all_of(rs_send.at[slot], out_send_sem.at[out_kinds[slot]])
    all_of(rs_send.at[0, :, 0 : 7 * TOK], out_send_sem.at[0])
    for stage in range(3):
        forward(stage).wait_send()
    for which in range(2):
        all_of(kv.at[1:8, which], ring_send_sem.at[which])
        all_of(rs.at[0:4, which], rs_send_sem.at[which])


def owner_sums(dq_parts, kv_parts, dq_out, dk_out, dv_out):
    for t in range(2):
        for r in range(0, HQ * D, 512):
            cols = slice(r, r + 512)
            total = dq_parts[0, t, :, cols].astype(F32) + dq_parts[1, t, :, cols].astype(F32)
            dq_out[t * SUB : (t + 1) * SUB, cols] = total.astype(BF)
    sums = []
    for which in range(2):
        total = jnp.zeros((TOK, KVH * D), F32)
        for kind in range(4):
            for hh in range(2):
                total = total + kv_parts[kind, hh, which].astype(F32)
        sums.append(total)
    dk_out[...] = (sums[0] * SCALE).astype(BF)
    dv_out[...] = sums[1].astype(BF)


def shards(queries, key_heads, value_heads, outputs, out_grad, log_total, positions):
    vmem = pl.BlockSpec(memory_space=pltpu.VMEM)
    anywhere = pl.BlockSpec(memory_space=pl.ANY)
    dma = pltpu.SemaphoreType.DMA
    parts = pl.pallas_call(
        kernel,
        out_shape=(
            jax.ShapeDtypeStruct((2, 2, SUB, HQ * D), BF),
            jax.ShapeDtypeStruct((4, 2, 2, TOK, KVH * D), BF),
        ),
        in_specs=[anywhere] * 7,
        out_specs=(anywhere, anywhere),
        scratch_shapes=[
            pltpu.VMEM((TOK, HQ * D), BF),
            pltpu.VMEM((TOK, KVH * D), BF),
            pltpu.VMEM((TOK, KVH * D), BF),
            pltpu.VMEM((TOK, HQ * D), BF),
            pltpu.VMEM((TOK, HQ * D), BF),
            pltpu.VMEM((TOK, HQ), BF),
            pltpu.SMEM((32, 256), jnp.int32),
            pltpu.VMEM((16, 2, 2, 3 * SUB, D), BF),
            pltpu.VMEM((KVH, 2, TOK, D), BF),
            pltpu.VMEM((LOCAL, 2, PLANE, 3 * SUB, D), BF),
            pltpu.VMEM((D, HALF), BF),
            pltpu.VMEM((LOCAL, 2, 2 * D, HALF), BF),
            pltpu.VMEM((LOCAL, 2, 2 * D, HALF), BF),
            pltpu.VMEM((2, 8, HALF), jnp.int32),
            pltpu.VMEM((Z, 2, PART, D), BF),
            pltpu.VMEM((Z, 2, PART, D), F32),
            pltpu.VMEM((LOCAL, 2, D, HALF), F32),
            pltpu.VMEM((2, 2, PLANE, SUB, D), BF),
            pltpu.VMEM((2, 2, D, HALF), BF),
            pltpu.VMEM((2, 2, D, HALF), BF),
            pltpu.VMEM((Z, 2, PART, D), BF),
            pltpu.VMEM((Z, 2, PART, D), BF),
            dma((7,)),
            dma((3,)),
            dma((3,)),
            dma((3,)),
            dma((3,)),
            dma,
            dma,
            dma((2,)),
            dma((2, Z)),
            dma((2,)),
            dma((2, Z)),
            dma((2,)),
            dma((2,)),
            dma((2,)),
            dma,
            dma((4,)),
            dma,
        ],
        compiler_params=pltpu.CompilerParams(
            collective_id=0, has_side_effects=True, vmem_limit_bytes=60 << 20
        ),
    )(queries, key_heads, value_heads, outputs, out_grad, log_total, positions)
    return pl.pallas_call(
        owner_sums,
        out_shape=(
            jax.ShapeDtypeStruct((TOK, HQ * D), BF),
            jax.ShapeDtypeStruct((TOK, KVH * D), BF),
            jax.ShapeDtypeStruct((TOK, KVH * D), BF),
        ),
        in_specs=[vmem, vmem],
        out_specs=(vmem, vmem, vmem),
    )(*parts)


def solution(mesh):
    spec = P(("head", "blk"), None)
    return jax.shard_map(
        shards,
        mesh=mesh,
        in_specs=(spec,) * 6 + (P(),),
        out_specs=(spec,) * 3,
        check_vma=False,
    )
```
